32 devices in a mesh: rows: 32 (over z, y, x, core).
Axes of the slice: x: 2, y: 2, z: 4, core: 2. Of those that a mesh axis runs over, the one named last changes fastest.
Arguments:
- signal: bfloat16 [32768, 256], P('rows'), may hold values from -6 to 6
- leaves: bfloat16 [32768, 512], P('rows'), may hold values from -0.25 to 0.25
- bases: bfloat16 [4, 32768, 128], P(None, 'rows'), may hold values from -6 to 6
- couplings: bfloat16 [15, 128, 128], replicated, may hold values from -0.5 to 0.5
- weights: float32 [32768], P('rows'), may hold values from 0.25 to 4
Outputs:
- result: bfloat16 [32768, 256], P('rows')
The draws below stay inside these ranges and needn't reach their ends.
All inputs are finite; a program needn't handle non-finite values.
Results may differ from the reference program's by a relative error of at most 0.007.
Values sent between devices are 32-bit elements; how exact they have to be, the bound alone decides.
No kernel may reach another device: no remote copies, remote signals or barrier semaphores. Data moves between devices by JAX's collectives and lax.ppermute only.
A program may use at most 64 MiB of HBM per device.

```python
import math
import jax
import jax.numpy as jnp
from jax import lax

NRHS = 256
LEAF = 512
R = 128
LEVELS = 4
N = 32768


def block_levels(rng, shape, shards, low, top_value):
    factor_of = 1.0
    for dim, shards_of in shards:
        draws = jax.random.uniform(jax.random.fold_in(jax.random.fold_in(rng, 6), dim), (shards_of,), jnp.float32, low / len(shards), top_value / len(shards))
        factor_of = factor_of * jnp.repeat(jnp.exp(draws), shape[dim] // shards_of).reshape((-1,) + (1,) * (len(shape) - 1 - dim))
    return factor_of


def scatter_about(stream_key, dims, scale, most, cuts=(), kind=jnp.bfloat16):
    values = jax.random.normal(stream_key, dims, jnp.float32) * scale
    if len(cuts) > 0:
        values = block_levels(stream_key, dims, cuts, -0.22, 0.18) * values
    return jnp.clip(values, min=-most, max=most).astype(kind)


def setup_inputs(seed: int = 0) -> dict:
    arg_keys = jax.random.split(jax.random.key(seed), 6)
    signal = scatter_about(arg_keys[0], (N, NRHS), 1.0, 6.0, ((0, 32),))
    leaves = scatter_about(arg_keys[1], (N, LEAF), LEAF ** -0.5, 0.25, ((0, 32),))
    bases = scatter_about(arg_keys[2], (LEVELS, N, R), 1.0, 6.0, ((1, 32),))
    couplings = scatter_about(arg_keys[3], (2 ** LEVELS - 1, R, R), R ** -0.5, 0.5)
    weights = jnp.clip(jnp.exp(math.log(4.0) - 2.7725887 * jax.random.uniform(arg_keys[4], (N,), jnp.float32) ** block_levels(arg_keys[4], (N,), ((0, 32),), -0.2, 0.2)), 0.25, 4.0)
    return dict(signal=signal, leaves=leaves, bases=bases, couplings=couplings, weights=weights)


def kernel_apply(vec, leaves, bases, couplings):
    total = vec.shape[0]
    width = vec.shape[1]
    count = total // LEAF
    blocks = leaves.reshape(count, LEAF, LEAF)
    parts = vec.reshape(count, LEAF, width)
    leaf_out = lax.map(lambda pair: jnp.dot(pair[0], pair[1], preferred_element_type=jnp.float32), (blocks, parts))
    result = leaf_out.reshape(total, width)
    for level in range(LEVELS):
        nodes = 2 ** (level + 1)
        size = total // nodes
        factor = 1.0 / math.sqrt(size * R)
        node_bases = bases[level].reshape(nodes, size, R)
        node_vecs = vec.reshape(nodes, size, width)
        proj = [jnp.dot(node_bases[k].T, node_vecs[k], preferred_element_type=jnp.float32) for k in range(nodes)]
        pieces = []
        for pair_idx in range(nodes // 2):
            coupling = couplings[nodes // 2 - 1 + pair_idx]
            left_q = (proj[2 * pair_idx + 1] * factor).astype(jnp.bfloat16)
            right_q = (proj[2 * pair_idx] * factor).astype(jnp.bfloat16)
            left_c = jnp.dot(coupling, left_q, preferred_element_type=jnp.float32).astype(jnp.bfloat16)
            right_c = jnp.dot(coupling.T, right_q, preferred_element_type=jnp.float32).astype(jnp.bfloat16)
            pieces.append(jnp.dot(node_bases[2 * pair_idx], left_c, preferred_element_type=jnp.float32))
            pieces.append(jnp.dot(node_bases[2 * pair_idx + 1], right_c, preferred_element_type=jnp.float32))
        result = result + jnp.concatenate(pieces, axis=0)
    return result

def reference(signal, leaves, bases, couplings, weights):
    first = kernel_apply(signal, leaves, bases, couplings)
    scaled = (weights[:, None] * first).astype(jnp.bfloat16)
    return kernel_apply(scaled, leaves, bases, couplings).astype(jnp.bfloat16)
```

```python
import functools
import math

import jax
import jax.numpy as jnp
from jax import lax
from jax.experimental import pallas as pl
from jax.experimental.pallas import tpu as pltpu
from jax.sharding import PartitionSpec as P

LEAF = 512
F32 = jnp.float32
BF16 = jnp.bfloat16


def in_vmem(count):
    return [pl.BlockSpec(memory_space=pltpu.VMEM)] * count


def call(kernel, outs, scalars, arrays, flops):
    moved = sum(math.prod(a.shape) * a.dtype.itemsize for a in (*arrays, *outs))
    return pl.pallas_call(
        kernel,
        out_shape=outs,
        in_specs=[pl.BlockSpec(memory_space=pltpu.SMEM)] + in_vmem(len(arrays)),
        out_specs=in_vmem(len(outs)),
        compiler_params=pltpu.CompilerParams(vmem_limit_bytes=24 * 2**20),
        cost_estimate=pl.CostEstimate(flops=flops, bytes_accessed=moved, transcendentals=0),
    )(scalars, *arrays)


def side_by_side(bases_ref, first, second):
    return jnp.concatenate([bases_ref[first], bases_ref[second]], axis=1)


def projections(bases_ref, parity, vec, out_ref):
    both = side_by_side(bases_ref, parity, parity + 2)
    proj = lax.dot_general(both, vec, (((0,), (0,)), ((), ())), preferred_element_type=F32)
    rank = bases_ref.shape[2]
    out_ref[0] = proj[:rank]
    out_ref[1] = proj[rank:]


def project_kernel(flip, ids_ref, bases_ref, vec_ref, out_ref):
    parity = ids_ref[0]
    projections(bases_ref, 1 - parity if flip else parity, vec_ref[...], out_ref)


def coefficients(ids_ref, couplings_ref, level, sums, factors):
    quotient = (sums * factors[level]).astype(BF16)
    coupling = couplings_ref[ids_ref[1 + level]]
    oriented = jnp.where(ids_ref[5 + level] == 0, coupling.astype(F32), coupling.astype(F32).T)
    return jnp.dot(oriented.astype(BF16), quotient, preferred_element_type=F32).astype(BF16)


def both_coefficients(ids_ref, couplings_ref, slot, own, other, factors):
    odd = ids_ref[0] == 1
    lower = coefficients(ids_ref, couplings_ref, 2 * slot, jnp.where(odd, own, other), factors)
    upper = coefficients(ids_ref, couplings_ref, 2 * slot + 1, jnp.where(odd, other, own), factors)
    return jnp.concatenate([lower, upper], axis=0)


def local_kernel(factors, ids_ref, couplings_ref, own_ref, other_ref, bases_ref, leaves_ref, vec_ref, part_ref):
    coeffs = both_coefficients(ids_ref, couplings_ref, 1, own_ref[...], other_ref[...], factors)
    for leaf in range(vec_ref.shape[0] // LEAF):
        rows = pl.ds(leaf * LEAF, LEAF)
        near = jnp.dot(leaves_ref[rows, :], vec_ref[rows, :], preferred_element_type=F32)
        basis = jnp.concatenate([bases_ref[2, rows, :], bases_ref[3, rows, :]], axis=1)
        part_ref[rows, :] = near + jnp.dot(basis, coeffs, preferred_element_type=F32)


def far(ids_ref, couplings_ref, own_ref, other_ref, bases_ref, part_ref, factors):
    coeffs = both_coefficients(ids_ref, couplings_ref, 0, own_ref[...], other_ref[...], factors)
    return part_ref[...] + jnp.dot(side_by_side(bases_ref, 0, 1), coeffs, preferred_element_type=F32)


def scale_kernel(
    factors, ids_ref, couplings_ref, own_ref, other_ref, bases_ref, part_ref, weights_ref, scaled_ref, send_ref
):
    first = far(ids_ref, couplings_ref, own_ref, other_ref, bases_ref, part_ref, factors)
    columns = weights_ref[...].T
    span = weights_ref.shape[1]
    for block in range(weights_ref.shape[0]):
        rows = slice(block * span, (block + 1) * span)
        scaled_ref[rows, :] = (columns[:, block : block + 1] * first[rows]).astype(BF16)
    projections(bases_ref, ids_ref[0], scaled_ref[...], send_ref)


def result_kernel(factors, ids_ref, couplings_ref, own_ref, other_ref, bases_ref, part_ref, result_ref):
    total = far(ids_ref, couplings_ref, own_ref, other_ref, bases_ref, part_ref, factors)
    result_ref[...] = total.astype(BF16)


def on_device(signal, leaves, bases, couplings, weights):
    count = lax.axis_size("rows")
    bits = count.bit_length() - 1
    myself = lax.axis_index("rows")
    rows_dev, width = signal.shape
    levels, _, rank = bases.shape
    odd = myself % 2 == 1
    far1, far2, far3, far4 = (1 << (bits - level - 1) for level in range(levels))
    factors = [1.0 / math.sqrt(rows_dev * (count >> level + 1) * rank) for level in range(levels)]
    ids = jnp.stack(
        [myself % 2]
        + [(1 << level) - 1 + (myself >> bits - level) for level in range(levels)]
        + [myself >> bits - level - 1 & 1 for level in range(levels)]
    ).astype(jnp.int32)
    span = 128
    weight_rows = weights.reshape(rows_dev // span, span)
    mults = rows_dev * width * rank * 2

    def swap(value, odd_mask, even_mask):
        pairs = [(source, source ^ (odd_mask if source % 2 else even_mask)) for source in range(count)]
        return lax.ppermute(value, "rows", pairs)

    def project(vec, flip):
        (out,) = call(
            functools.partial(project_kernel, flip),
            [jax.ShapeDtypeStruct((2, rank, width), F32)],
            ids,
            [bases, vec],
            2 * mults,
        )
        return out

    def siblings(send, keep):
        sums = keep + swap(send, 1, 1)
        for bit in range(1, bits - levels):
            sums = sums + swap(sums, 1 << bit, 1 << bit)
        high, low = sums[0], sums[1]
        high = high + swap(high, far4, far3)
        low = swap(low, far3, far4)
        high = high + swap(high, far3, far4)
        low = jnp.where(odd, low + swap(low, far4, 0), low)
        got = swap(high, far2, far2)
        high = jnp.where(odd, high + got, got)
        high = swap(high, far1, 0)
        return (high, swap(high, 1, 1)), (low, swap(low, 1, 1))

    def local(vec, low):
        (part,) = call(
            functools.partial(local_kernel, factors),
            [jax.ShapeDtypeStruct((rows_dev, width), F32)],
            ids,
            [couplings, *low, bases, leaves, vec],
            (2 + LEAF // rank) * mults,
        )
        return part

    high, low = siblings(project(signal, False), project(signal, True))
    scaled, send = call(
        functools.partial(scale_kernel, factors),
        [jax.ShapeDtypeStruct((rows_dev, width), BF16), jax.ShapeDtypeStruct((2, rank, width), F32)],
        ids,
        [couplings, *high, bases, local(signal, low), weight_rows],
        4 * mults,
    )
    high, low = siblings(send, project(scaled, True))
    (result,) = call(
        functools.partial(result_kernel, factors),
        [jax.ShapeDtypeStruct((rows_dev, width), BF16)],
        ids,
        [couplings, *high, bases, local(scaled, low)],
        2 * mults,
    )
    return result


def solution(mesh):
    in_specs = (P("rows", None), P("rows", None), P(None, "rows", None), P(), P("rows"))
    out_specs = P("rows", None)
    return jax.shard_map(
        on_device, mesh=mesh, in_specs=in_specs, out_specs=out_specs, check_vma=False
    )
```

```python
import functools
import math

import jax
import jax.numpy as jnp
from jax import lax
from jax.experimental import pallas as pl
from jax.experimental.pallas import tpu as pltpu
from jax.sharding import PartitionSpec as P

LEAF = 512
CHUNK = 256
SPAN = 128
F32 = jnp.float32
BF16 = jnp.bfloat16


VMEM = pl.BlockSpec(memory_space=pltpu.VMEM)
SMEM = pl.BlockSpec(memory_space=pltpu.SMEM)
HBM = pl.BlockSpec(memory_space=pltpu.HBM)


def call(kernel, outs, scalars, arrays, flops, arrays_in=VMEM, outs_in=VMEM, scratch=()):
    moved = sum(math.prod(a.shape) * a.dtype.itemsize for a in (*arrays, *outs))
    return pl.pallas_call(
        kernel,
        out_shape=outs,
        in_specs=[SMEM] + [arrays_in] * len(arrays),
        out_specs=[outs_in] * len(outs),
        scratch_shapes=scratch,
        compiler_params=pltpu.CompilerParams(vmem_limit_bytes=24 * 2**20),
        cost_estimate=pl.CostEstimate(flops=flops, bytes_accessed=moved, transcendentals=0),
    )(scalars, *arrays)


def transposed_dot(basis, vec):
    return lax.dot_general(basis, vec, (((0,), (0,)), ((), ())), preferred_element_type=F32)


def first_kernel(ids_ref, bases_ref, vec_ref, out_ref, bases_buf, vec_buf, sems):
    parity = ids_ref[0]
    rank = bases_ref.shape[2]
    copies = []
    for chunk in range(vec_ref.shape[0] // CHUNK):
        rows = pl.ds(chunk * CHUNK, CHUNK)
        own = [pltpu.make_async_copy(vec_ref.at[rows, :], vec_buf.at[rows, :], sems.at[chunk, 0])]
        for slot in range(2):
            source = bases_ref.at[parity + 2 * slot, rows, :]
            target = bases_buf.at[rows, pl.ds(slot * rank, rank)]
            own.append(pltpu.make_async_copy(source, target, sems.at[chunk, 1 + slot]))
        for copy in own:
            copy.start()
        copies.append(own)
    total = None
    for chunk, own in enumerate(copies):
        for copy in own:
            copy.wait()
        rows = slice(chunk * CHUNK, (chunk + 1) * CHUNK)
        term = transposed_dot(bases_buf[rows, :], vec_buf[rows, :])
        total = term if total is None else total + term
    out_ref[0] = total[:rank]
    out_ref[1] = total[rank:]


def kept_kernel(ids_ref, bases_ref, vec_ref, high_ref, low_ref):
    other = 1 - ids_ref[0]
    rank = bases_ref.shape[2]
    both = jnp.concatenate([bases_ref[other], bases_ref[other + 2]], axis=1)
    proj = transposed_dot(both, vec_ref[...])
    high_ref[...] = proj[:rank]
    low_ref[...] = proj[rank:]


def prepare_kernel(ids_ref, couplings_ref, bases_ref, oriented_ref, turned_ref):
    for level in range(bases_ref.shape[0]):
        coupling = couplings_ref[ids_ref[1 + level]].astype(F32)
        oriented_ref[level] = jnp.where(ids_ref[5 + level] == 0, coupling, coupling.T).astype(BF16)
        turned_ref[level] = bases_ref[level].T


def coefficients(ids_ref, oriented_ref, level, own, other, factors):
    odd = ids_ref[0] == 1
    pieces = []
    for step, sums in enumerate((jnp.where(odd, own, other), jnp.where(odd, other, own))):
        quotient = (sums * factors[level + step]).astype(BF16)
        coeffs = jnp.dot(oriented_ref[level + step], quotient, preferred_element_type=F32)
        pieces.append(coeffs.astype(BF16))
    return jnp.concatenate(pieces, axis=0)


def expanded(bases_ref, level, rows, coeffs):
    basis = jnp.concatenate([bases_ref[level, rows, :], bases_ref[level + 1, rows, :]], axis=1)
    return jnp.dot(basis, coeffs, preferred_element_type=F32)


def local_kernel(factors, ids_ref, oriented_ref, own_ref, other_ref, bases_ref, leaves_ref, vec_ref, part_ref):
    coeffs = coefficients(ids_ref, oriented_ref, 2, own_ref[...], other_ref[...], factors)
    for leaf in range(vec_ref.shape[0] // LEAF):
        rows = pl.ds(leaf * LEAF, LEAF)
        near = jnp.dot(leaves_ref[rows, :], vec_ref[rows, :], preferred_element_type=F32)
        part_ref[rows, :] = near + expanded(bases_ref, 2, rows, coeffs)


def scale_kernel(
    factors, ids_ref, oriented_ref, own_ref, other_ref, bases_ref, part_ref, turned_ref, weights_ref, scaled_ref, send_ref
):
    coeffs = coefficients(ids_ref, oriented_ref, 0, own_ref[...], other_ref[...], factors)
    columns = weights_ref[...].T
    parity = ids_ref[0]
    rank = bases_ref.shape[2]
    total = None
    for chunk in range(part_ref.shape[0] // CHUNK):
        rows = pl.ds(chunk * CHUNK, CHUNK)
        first = part_ref[rows, :] + expanded(bases_ref, 0, rows, coeffs)
        blocks = range(chunk * CHUNK // SPAN, (chunk + 1) * CHUNK // SPAN)
        column = jnp.concatenate([columns[:, block : block + 1] for block in blocks], axis=0)
        scaled = (column * first).astype(BF16)
        scaled_ref[rows, :] = scaled
        turned = jnp.concatenate([turned_ref[parity, :, rows], turned_ref[parity + 2, :, rows]], axis=0)
        term = jnp.dot(turned, scaled, preferred_element_type=F32)
        total = term if total is None else total + term
    send_ref[0] = total[:rank]
    send_ref[1] = total[rank:]


def kept_again_kernel(ids_ref, turned_ref, vec_ref, high_ref, low_ref):
    other = 1 - ids_ref[0]
    vec = vec_ref[...]
    high_ref[...] = jnp.dot(turned_ref[other], vec, preferred_element_type=F32)
    low_ref[...] = jnp.dot(turned_ref[other + 2], vec, preferred_element_type=F32)


def result_kernel(factors, ids_ref, oriented_ref, own_ref, other_ref, bases_ref, part_ref, result_ref, buf, sems):
    coeffs = coefficients(ids_ref, oriented_ref, 0, own_ref[...], other_ref[...], factors)
    copies = []
    for chunk in range(part_ref.shape[0] // CHUNK):
        rows = pl.ds(chunk * CHUNK, CHUNK)
        total = part_ref[rows, :] + expanded(bases_ref, 0, rows, coeffs)
        buf[rows, :] = total.astype(BF16)
        copies.append(pltpu.make_async_copy(buf.at[rows, :], result_ref.at[rows, :], sems.at[chunk]))
        copies[-1].start()
    for copy in copies:
        copy.wait()


def on_device(signal, leaves, bases, couplings, weights):
    count = lax.axis_size("rows")
    bits = count.bit_length() - 1
    myself = lax.axis_index("rows")
    rows_dev, width = signal.shape
    levels, _, rank = bases.shape
    odd = myself % 2 == 1
    far1, far2, far3, far4 = (1 << (bits - level - 1) for level in range(levels))
    factors = [1.0 / math.sqrt(rows_dev * (count >> level + 1) * rank) for level in range(levels)]
    ids = jnp.stack(
        [myself % 2]
        + [(1 << level) - 1 + (myself >> bits - level) for level in range(levels)]
        + [myself >> bits - level - 1 & 1 for level in range(levels)]
    ).astype(jnp.int32)
    weight_rows = weights.reshape(rows_dev // SPAN, SPAN)
    mults = rows_dev * width * rank * 2
    chunks = rows_dev // CHUNK
    sums_shape = jax.ShapeDtypeStruct((rank, width), F32)
    pair_shape = jax.ShapeDtypeStruct((2, rank, width), F32)
    part_shape = jax.ShapeDtypeStruct((rows_dev, width), F32)
    vec_shape = jax.ShapeDtypeStruct((rows_dev, width), BF16)

    def swap(value, odd_mask, even_mask):
        pairs = [(source, source ^ (odd_mask if source % 2 else even_mask)) for source in range(count)]
        return lax.ppermute(value, "rows", pairs)

    def siblings(send, high, low):
        got = swap(send, 1, 1)
        high = high + got[0]
        low = low + got[1]
        for bit in range(1, bits - levels):
            high = high + swap(high, 1 << bit, 1 << bit)
            low = low + swap(low, 1 << bit, 1 << bit)
        near = swap(high, far1, far2)
        across = swap(high, far1 | far2, far4)
        high = jnp.where(odd, near + across, near)
        low = swap(low, far3, far4)
        high = high + swap(high, far4, far3)
        low = jnp.where(odd, low + swap(low, far4, far4), low)
        high = high + swap(high, far3, far4)
        return (high, swap(high, 1, 1)), (low, swap(low, 1, 1))

    def local(vec, low):
        (part,) = call(
            functools.partial(local_kernel, factors),
            [part_shape],
            ids,
            [oriented, *low, bases, leaves, vec],
            (2 + LEAF // rank) * mults,
        )
        return part

    (send,) = call(
        first_kernel,
        [pair_shape],
        ids,
        [pltpu.with_memory_space_constraint(array, pltpu.HBM) for array in (bases, signal)],
        2 * mults,
        arrays_in=HBM,
        scratch=[
            pltpu.VMEM((rows_dev, 2 * rank), BF16),
            pltpu.VMEM((rows_dev, width), BF16),
            pltpu.SemaphoreType.DMA((chunks, 3)),
        ],
    )
    kept = call(kept_kernel, [sums_shape] * 2, ids, [bases, signal], 2 * mults)
    oriented, turned = call(
        prepare_kernel,
        [
            jax.ShapeDtypeStruct((levels, rank, rank), BF16),
            jax.ShapeDtypeStruct((levels, rank, rows_dev), BF16),
        ],
        ids,
        [couplings, bases],
        mults,
    )
    high, low = siblings(send, *kept)
    scaled, send = call(
        functools.partial(scale_kernel, factors),
        [vec_shape, pair_shape],
        ids,
        [oriented, *high, bases, local(signal, low), turned, weight_rows],
        4 * mults,
    )
    kept = call(kept_again_kernel, [sums_shape] * 2, ids, [turned, scaled], 2 * mults)
    high, low = siblings(send, *kept)
    (result,) = call(
        functools.partial(result_kernel, factors),
        [vec_shape],
        ids,
        [oriented, *high, bases, local(scaled, low)],
        2 * mults,
        outs_in=HBM,
        scratch=[pltpu.VMEM((rows_dev, width), BF16), pltpu.SemaphoreType.DMA((chunks,))],
    )
    return result


def solution(mesh):
    in_specs = (P("rows", None), P("rows", None), P(None, "rows", None), P(), P("rows"))
    out_specs = P("rows", None)
    return jax.shard_map(
        on_device, mesh=mesh, in_specs=in_specs, out_specs=out_specs, check_vma=False
    )
```

```python
import functools
import math

import jax
import jax.numpy as jnp
from jax import lax
from jax.experimental import pallas as pl
from jax.experimental.pallas import tpu as pltpu
from jax.sharding import PartitionSpec as P

AXIS = "rows"
LEAF = 512
CHUNK = 256
SPAN = 128
F32 = jnp.float32
BF16 = jnp.bfloat16


VMEM = pl.BlockSpec(memory_space=pltpu.VMEM)
HBM = pl.BlockSpec(memory_space=pltpu.HBM)


def call(kernel, outs, arrays, flops, arrays_in=VMEM, outs_in=VMEM, scratch=()):
    moved = sum(math.prod(a.shape) * a.dtype.itemsize for a in (*arrays, *outs))
    return pl.pallas_call(
        kernel,
        out_shape=outs,
        in_specs=[arrays_in] * len(arrays),
        out_specs=[outs_in] * len(outs),
        scratch_shapes=scratch,
        compiler_params=pltpu.CompilerParams(vmem_limit_bytes=24 * 2**20),
        cost_estimate=pl.CostEstimate(flops=flops, bytes_accessed=moved, transcendentals=0),
    )(*arrays)


def index_bits():
    return lax.axis_size(AXIS).bit_length() - 1


def transposed_dot(basis, vec):
    return lax.dot_general(basis, vec, (((0,), (0,)), ((), ())), preferred_element_type=F32)


def first_kernel(bases_ref, vec_ref, out_ref, bases_buf, vec_buf, sems):
    parity = lax.axis_index(AXIS) % 2
    rank = bases_ref.shape[2]
    copies = []
    for chunk in range(vec_ref.shape[0] // CHUNK):
        rows = pl.ds(chunk * CHUNK, CHUNK)
        own = [pltpu.make_async_copy(vec_ref.at[rows, :], vec_buf.at[rows, :], sems.at[chunk, 0])]
        for slot in range(2):
            source = bases_ref.at[parity + 2 * slot, rows, :]
            target = bases_buf.at[rows, pl.ds(slot * rank, rank)]
            own.append(pltpu.make_async_copy(source, target, sems.at[chunk, 1 + slot]))
        for copy in own:
            copy.start()
        copies.append(own)
    total = None
    for chunk, own in enumerate(copies):
        for copy in own:
            copy.wait()
        rows = slice(chunk * CHUNK, (chunk + 1) * CHUNK)
        term = transposed_dot(bases_buf[rows, :], vec_buf[rows, :])
        total = term if total is None else total + term
    out_ref[0] = total[:rank]
    out_ref[1] = total[rank:]


def kept_kernel(bases_ref, vec_ref, high_ref, low_ref):
    other = 1 - lax.axis_index(AXIS) % 2
    rank = bases_ref.shape[2]
    both = jnp.concatenate([bases_ref[other], bases_ref[other + 2]], axis=1)
    proj = transposed_dot(both, vec_ref[...])
    high_ref[...] = proj[:rank]
    low_ref[...] = proj[rank:]


def prepare_kernel(couplings_ref, bases_ref, oriented_ref, turned_ref):
    myself = lax.axis_index(AXIS)
    bits = index_bits()
    for level in range(bases_ref.shape[0]):
        coupling = couplings_ref[(1 << level) - 1 + (myself >> bits - level)].astype(F32)
        side = myself >> bits - level - 1 & 1
        oriented_ref[level] = jnp.where(side == 0, coupling, coupling.T).astype(BF16)
        turned_ref[level] = bases_ref[level].T


def coefficients(oriented_ref, level, own, other, factors):
    odd = lax.axis_index(AXIS) % 2 == 1
    pieces = []
    for step, sums in enumerate((jnp.where(odd, own, other), jnp.where(odd, other, own))):
        quotient = (sums * factors[level + step]).astype(BF16)
        coeffs = jnp.dot(oriented_ref[level + step], quotient, preferred_element_type=F32)
        pieces.append(coeffs.astype(BF16))
    return jnp.concatenate(pieces, axis=0)


def expanded(bases_ref, level, rows, coeffs):
    basis = jnp.concatenate([bases_ref[level, rows, :], bases_ref[level + 1, rows, :]], axis=1)
    return jnp.dot(basis, coeffs, preferred_element_type=F32)


def local_kernel(factors, oriented_ref, own_ref, other_ref, bases_ref, leaves_ref, vec_ref, part_ref):
    coeffs = coefficients(oriented_ref, 2, own_ref[...], other_ref[...], factors)
    for leaf in range(vec_ref.shape[0] // LEAF):
        rows = pl.ds(leaf * LEAF, LEAF)
        near = jnp.dot(leaves_ref[rows, :], vec_ref[rows, :], preferred_element_type=F32)
        part_ref[rows, :] = near + expanded(bases_ref, 2, rows, coeffs)


def scale_kernel(
    factors, oriented_ref, own_ref, other_ref, bases_ref, part_ref, turned_ref, weights_ref, scaled_ref, send_ref
):
    coeffs = coefficients(oriented_ref, 0, own_ref[...], other_ref[...], factors)
    columns = weights_ref[...].T
    parity = lax.axis_index(AXIS) % 2
    rank = bases_ref.shape[2]
    total = None
    for chunk in range(part_ref.shape[0] // CHUNK):
        rows = pl.ds(chunk * CHUNK, CHUNK)
        first = part_ref[rows, :] + expanded(bases_ref, 0, rows, coeffs)
        blocks = range(chunk * CHUNK // SPAN, (chunk + 1) * CHUNK // SPAN)
        column = jnp.concatenate([columns[:, block : block + 1] for block in blocks], axis=0)
        scaled = (column * first).astype(BF16)
        scaled_ref[rows, :] = scaled
        turned = jnp.concatenate([turned_ref[parity, :, rows], turned_ref[parity + 2, :, rows]], axis=0)
        term = jnp.dot(turned, scaled, preferred_element_type=F32)
        total = term if total is None else total + term
    send_ref[0] = total[:rank]
    send_ref[1] = total[rank:]


def kept_again_kernel(turned_ref, vec_ref, high_ref, low_ref):
    other = 1 - lax.axis_index(AXIS) % 2
    vec = vec_ref[...]
    high_ref[...] = jnp.dot(turned_ref[other], vec, preferred_element_type=F32)
    low_ref[...] = jnp.dot(turned_ref[other + 2], vec, preferred_element_type=F32)


def result_kernel(factors, oriented_ref, own_ref, other_ref, bases_ref, part_ref, result_ref, buf, sems):
    coeffs = coefficients(oriented_ref, 0, own_ref[...], other_ref[...], factors)
    copies = []
    for chunk in range(part_ref.shape[0] // CHUNK):
        rows = pl.ds(chunk * CHUNK, CHUNK)
        total = part_ref[rows, :] + expanded(bases_ref, 0, rows, coeffs)
        buf[rows, :] = total.astype(BF16)
        copies.append(pltpu.make_async_copy(buf.at[rows, :], result_ref.at[rows, :], sems.at[chunk]))
        copies[-1].start()
    for copy in copies:
        copy.wait()


def on_device(signal, leaves, bases, couplings, weights):
    count = lax.axis_size(AXIS)
    bits = index_bits()
    rows_dev, width = signal.shape
    levels, _, rank = bases.shape
    odd = lax.axis_index(AXIS) % 2 == 1
    far1, far2, far3, far4 = (1 << (bits - level - 1) for level in range(levels))
    factors = [1.0 / math.sqrt(rows_dev * (count >> level + 1) * rank) for level in range(levels)]
    weight_rows = weights.reshape(rows_dev // SPAN, SPAN)
    mults = rows_dev * width * rank * 2
    chunks = rows_dev // CHUNK
    sums_shape = jax.ShapeDtypeStruct((rank, width), F32)
    pair_shape = jax.ShapeDtypeStruct((2, rank, width), F32)
    part_shape = jax.ShapeDtypeStruct((rows_dev, width), F32)
    vec_shape = jax.ShapeDtypeStruct((rows_dev, width), BF16)

    def swap(value, odd_mask, even_mask):
        pairs = [(source, source ^ (odd_mask if source % 2 else even_mask)) for source in range(count)]
        return lax.ppermute(value, AXIS, pairs)

    def siblings(send, high, low, riders=()):
        got = swap(send, 1, 1)
        high = high + got[0]
        low = low + got[1]
        for bit in range(1, bits - levels):
            high = high + swap(high, 1 << bit, 1 << bit)
            low = low + swap(low, 1 << bit, 1 << bit)
        near = swap(high, far1, far2)
        across = swap(high, far1 | far2, far4)
        near, across, *riders = lax.optimization_barrier((near, across, *riders))
        high = jnp.where(odd, near + across, near)
        low = swap(low, far3, far4)
        high = high + swap(high, far4, far3)
        low = jnp.where(odd, low + swap(low, far4, far4), low)
        high = high + swap(high, far3, far4)
        return (high, swap(high, 1, 1)), (low, swap(low, 1, 1)), *riders

    def local(vec, low):
        (part,) = call(
            functools.partial(local_kernel, factors),
            [part_shape],
                [oriented, *low, bases, leaves, vec],
            (2 + LEAF // rank) * mults,
        )
        return part

    (send,) = call(
        first_kernel,
        [pair_shape],
        [pltpu.with_memory_space_constraint(array, pltpu.HBM) for array in (bases, signal)],
        2 * mults,
        arrays_in=HBM,
        scratch=[
            pltpu.VMEM((rows_dev, 2 * rank), BF16),
            pltpu.VMEM((rows_dev, width), BF16),
            pltpu.SemaphoreType.DMA((chunks, 3)),
        ],
    )
    kept = call(kept_kernel, [sums_shape] * 2, [bases, signal], 2 * mults)
    prepared = call(
        prepare_kernel,
        [
            jax.ShapeDtypeStruct((levels, rank, rank), BF16),
            jax.ShapeDtypeStruct((levels, rank, rows_dev), BF16),
        ],
        [couplings, bases],
        mults,
    )
    high, low, oriented, turned = siblings(send, *kept, prepared)
    scaled, send = call(
        functools.partial(scale_kernel, factors),
        [vec_shape, pair_shape],
        [oriented, *high, bases, local(signal, low), turned, weight_rows],
        4 * mults,
    )
    kept = call(kept_again_kernel, [sums_shape] * 2, [turned, scaled], 2 * mults)
    high, low = siblings(send, *kept)
    (result,) = call(
        functools.partial(result_kernel, factors),
        [vec_shape],
        [oriented, *high, bases, local(scaled, low)],
        2 * mults,
        outs_in=HBM,
        scratch=[pltpu.VMEM((rows_dev, width), BF16), pltpu.SemaphoreType.DMA((chunks,))],
    )
    return result


def solution(mesh):
    in_specs = (P("rows", None), P("rows", None), P(None, "rows", None), P(), P("rows"))
    out_specs = P("rows", None)
    return jax.shard_map(
        on_device, mesh=mesh, in_specs=in_specs, out_specs=out_specs, check_vma=False
    )
```

```python
import functools
import math

import jax
import jax.numpy as jnp
from jax import lax
from jax.experimental import pallas as pl
from jax.experimental.pallas import tpu as pltpu
from jax.sharding import PartitionSpec as P

AXIS = "rows"
LEAF = 512
CHUNK = 256
SPAN = 128
F32 = jnp.float32
BF16 = jnp.bfloat16


VMEM = pl.BlockSpec(memory_space=pltpu.VMEM)
HBM = pl.BlockSpec(memory_space=pltpu.HBM)


def call(kernel, outs, arrays, flops, arrays_in=VMEM, outs_in=VMEM, scratch=()):
    moved = sum(math.prod(a.shape) * a.dtype.itemsize for a in (*arrays, *outs))
    return pl.pallas_call(
        kernel,
        out_shape=outs,
        in_specs=[arrays_in] * len(arrays),
        out_specs=[outs_in] * len(outs),
        scratch_shapes=scratch,
        compiler_params=pltpu.CompilerParams(vmem_limit_bytes=24 * 2**20),
        cost_estimate=pl.CostEstimate(flops=flops, bytes_accessed=moved, transcendentals=0),
    )(*arrays)


def index_bits():
    return lax.axis_size(AXIS).bit_length() - 1


def transposed_dot(basis, vec):
    return lax.dot_general(basis, vec, (((0,), (0,)), ((), ())), preferred_element_type=F32)


def first_kernel(bases_in, vec_in, out_ref, bases_ref, vec_ref, sems):
    parity = lax.axis_index(AXIS) % 2
    rank = bases_in.shape[2]
    rows_dev = vec_in.shape[0]
    chunks = rows_dev // CHUNK

    def basis_copy(level, rows, sem):
        return pltpu.make_async_copy(bases_in.at[level, rows, :], bases_ref.at[level, rows, :], sem)

    copies = []
    for chunk in range(chunks):
        rows = pl.ds(chunk * CHUNK, CHUNK)
        copies.append([pltpu.make_async_copy(vec_in.at[rows, :], vec_ref.at[rows, :], sems.at[chunk, 0])])
        copies[-1] += [basis_copy(parity + 2 * slot, rows, sems.at[chunk, 1 + slot]) for slot in range(2)]
    copies.append([basis_copy(1 - parity + 2 * slot, pl.ds(0, rows_dev), sems.at[chunks, slot]) for slot in range(2)])
    for copy in sum(copies, []):
        copy.start()
    total = None
    for chunk in range(chunks):
        for copy in copies[chunk]:
            copy.wait()
        rows = pl.ds(chunk * CHUNK, CHUNK)
        basis = jnp.concatenate([bases_ref[parity, rows, :], bases_ref[parity + 2, rows, :]], axis=1)
        term = transposed_dot(basis, vec_ref[rows, :])
        total = term if total is None else total + term
    out_ref[0] = total[:rank]
    out_ref[1] = total[rank:]
    for copy in copies[chunks]:
        copy.wait()


def kept_kernel(bases_ref, vec_ref, high_ref, low_ref):
    other = 1 - lax.axis_index(AXIS) % 2
    rank = bases_ref.shape[2]
    both = jnp.concatenate([bases_ref[other], bases_ref[other + 2]], axis=1)
    proj = transposed_dot(both, vec_ref[...])
    high_ref[...] = proj[:rank]
    low_ref[...] = proj[rank:]


def prepare_kernel(couplings_ref, bases_ref, oriented_ref, turned_ref):
    myself = lax.axis_index(AXIS)
    bits = index_bits()
    for level in range(bases_ref.shape[0]):
        coupling = couplings_ref[(1 << level) - 1 + (myself >> bits - level)].astype(F32)
        side = myself >> bits - level - 1 & 1
        oriented_ref[level] = jnp.where(side == 0, coupling, coupling.T).astype(BF16)
        turned_ref[level] = bases_ref[level].T


def coefficients(oriented_ref, level, own, other, factors):
    odd = lax.axis_index(AXIS) % 2 == 1
    pieces = []
    for step, sums in enumerate((jnp.where(odd, own, other), jnp.where(odd, other, own))):
        quotient = (sums * factors[level + step]).astype(BF16)
        coeffs = jnp.dot(oriented_ref[level + step], quotient, preferred_element_type=F32)
        pieces.append(coeffs.astype(BF16))
    return jnp.concatenate(pieces, axis=0)


def expanded(bases_ref, level, rows, coeffs):
    basis = jnp.concatenate([bases_ref[level, rows, :], bases_ref[level + 1, rows, :]], axis=1)
    return jnp.dot(basis, coeffs, preferred_element_type=F32)


def local_kernel(factors, oriented_ref, own_ref, other_ref, bases_ref, leaves_ref, vec_ref, part_ref):
    coeffs = coefficients(oriented_ref, 2, own_ref[...], other_ref[...], factors)
    for leaf in range(vec_ref.shape[0] // LEAF):
        rows = pl.ds(leaf * LEAF, LEAF)
        near = jnp.dot(leaves_ref[rows, :], vec_ref[rows, :], preferred_element_type=F32)
        part_ref[rows, :] = near + expanded(bases_ref, 2, rows, coeffs)


def scale_kernel(
    factors, oriented_ref, own_ref, other_ref, bases_ref, part_ref, turned_ref, weights_ref, scaled_ref, send_ref
):
    coeffs = coefficients(oriented_ref, 0, own_ref[...], other_ref[...], factors)
    columns = weights_ref[...].T
    parity = lax.axis_index(AXIS) % 2
    rank = bases_ref.shape[2]
    total = None
    for chunk in range(part_ref.shape[0] // CHUNK):
        rows = pl.ds(chunk * CHUNK, CHUNK)
        first = part_ref[rows, :] + expanded(bases_ref, 0, rows, coeffs)
        blocks = range(chunk * CHUNK // SPAN, (chunk + 1) * CHUNK // SPAN)
        column = jnp.concatenate([columns[:, block : block + 1] for block in blocks], axis=0)
        scaled = (column * first).astype(BF16)
        scaled_ref[rows, :] = scaled
        turned = jnp.concatenate([turned_ref[parity, :, rows], turned_ref[parity + 2, :, rows]], axis=0)
        term = jnp.dot(turned, scaled, preferred_element_type=F32)
        total = term if total is None else total + term
    send_ref[0] = total[:rank]
    send_ref[1] = total[rank:]


def kept_again_kernel(turned_ref, vec_ref, high_ref, low_ref):
    other = 1 - lax.axis_index(AXIS) % 2
    vec = vec_ref[...]
    high_ref[...] = jnp.dot(turned_ref[other], vec, preferred_element_type=F32)
    low_ref[...] = jnp.dot(turned_ref[other + 2], vec, preferred_element_type=F32)


def result_kernel(factors, oriented_ref, own_ref, other_ref, bases_ref, part_ref, result_ref, buf, sems):
    coeffs = coefficients(oriented_ref, 0, own_ref[...], other_ref[...], factors)
    copies = []
    for chunk in range(part_ref.shape[0] // CHUNK):
        rows = pl.ds(chunk * CHUNK, CHUNK)
        total = part_ref[rows, :] + expanded(bases_ref, 0, rows, coeffs)
        buf[rows, :] = total.astype(BF16)
        copies.append(pltpu.make_async_copy(buf.at[rows, :], result_ref.at[rows, :], sems.at[chunk]))
        copies[-1].start()
    for copy in copies:
        copy.wait()


def on_device(signal, leaves, bases, couplings, weights):
    count = lax.axis_size(AXIS)
    bits = index_bits()
    rows_dev, width = signal.shape
    levels, _, rank = bases.shape
    odd = lax.axis_index(AXIS) % 2 == 1
    far1, far2, far3, far4 = (1 << (bits - level - 1) for level in range(levels))
    factors = [1.0 / math.sqrt(rows_dev * (count >> level + 1) * rank) for level in range(levels)]
    weight_rows = weights.reshape(rows_dev // SPAN, SPAN)
    mults = rows_dev * width * rank * 2
    chunks = rows_dev // CHUNK
    sums_shape = jax.ShapeDtypeStruct((rank, width), F32)
    pair_shape = jax.ShapeDtypeStruct((2, rank, width), F32)
    part_shape = jax.ShapeDtypeStruct((rows_dev, width), F32)
    vec_shape = jax.ShapeDtypeStruct((rows_dev, width), BF16)

    def swap(value, odd_mask, even_mask):
        pairs = [(source, source ^ (odd_mask if source % 2 else even_mask)) for source in range(count)]
        return lax.ppermute(value, AXIS, pairs)

    def siblings(send, high, low, riders=()):
        got = swap(send, 1, 1)
        high = high + got[0]
        low = low + got[1]
        for bit in range(1, bits - levels):
            high = high + swap(high, 1 << bit, 1 << bit)
            low = low + swap(low, 1 << bit, 1 << bit)
        near = swap(high, far1, far4)
        across = swap(high, far1 | far2, far3)
        near, across, *riders = lax.optimization_barrier((near, across, *riders))
        high = jnp.where(odd, near + across, high + near)
        low = swap(low, far3, far4)
        got = swap(high, far3, far2)
        high = jnp.where(odd, high + got, got)
        low = jnp.where(odd, low + swap(low, far4, far4), low)
        high = high + swap(high, far4, far3)
        return (high, swap(high, 1, 1)), (low, swap(low, 1, 1)), *riders

    def local(vec, low):
        (part,) = call(
            functools.partial(local_kernel, factors),
            [part_shape],
                [oriented, *low, bases, leaves, vec],
            (2 + LEAF // rank) * mults,
        )
        return part

    send, bases, signal = call(
        first_kernel,
        [
            pair_shape,
            jax.ShapeDtypeStruct(bases.shape, BF16),
            jax.ShapeDtypeStruct(signal.shape, BF16),
        ],
        [pltpu.with_memory_space_constraint(array, pltpu.HBM) for array in (bases, signal)],
        2 * mults,
        arrays_in=HBM,
        scratch=[pltpu.SemaphoreType.DMA((chunks + 1, 3))],
    )
    kept = call(kept_kernel, [sums_shape] * 2, [bases, signal], 2 * mults)
    prepared = call(
        prepare_kernel,
        [
            jax.ShapeDtypeStruct((levels, rank, rank), BF16),
            jax.ShapeDtypeStruct((levels, rank, rows_dev), BF16),
        ],
        [couplings, bases],
        mults,
    )
    high, low, oriented, turned = siblings(send, *kept, prepared)
    scaled, send = call(
        functools.partial(scale_kernel, factors),
        [vec_shape, pair_shape],
        [oriented, *high, bases, local(signal, low), turned, weight_rows],
        4 * mults,
    )
    kept = call(kept_again_kernel, [sums_shape] * 2, [turned, scaled], 2 * mults)
    high, low = siblings(send, *kept)
    (result,) = call(
        functools.partial(result_kernel, factors),
        [vec_shape],
        [oriented, *high, bases, local(scaled, low)],
        2 * mults,
        outs_in=HBM,
        scratch=[pltpu.VMEM((rows_dev, width), BF16), pltpu.SemaphoreType.DMA((chunks,))],
    )
    return result


def solution(mesh):
    in_specs = (P("rows", None), P("rows", None), P(None, "rows", None), P(), P("rows"))
    out_specs = P("rows", None)
    return jax.shard_map(
        on_device, mesh=mesh, in_specs=in_specs, out_specs=out_specs, check_vma=False
    )
```

```python
import functools
import math

import jax
import jax.numpy as jnp
from jax import lax
from jax.experimental import pallas as pl
from jax.experimental.pallas import tpu as pltpu
from jax.sharding import PartitionSpec as P

AXIS = "rows"
LEAF = 512
CHUNK = 256
SPAN = 128
F32 = jnp.float32
BF16 = jnp.bfloat16


VMEM = pl.BlockSpec(memory_space=pltpu.VMEM)
HBM = pl.BlockSpec(memory_space=pltpu.HBM)


def call(kernel, outs, arrays, flops, arrays_in=VMEM, outs_in=VMEM, scratch=()):
    moved = sum(math.prod(a.shape) * a.dtype.itemsize for a in (*arrays, *outs))
    return pl.pallas_call(
        kernel,
        out_shape=outs,
        in_specs=[arrays_in] * len(arrays),
        out_specs=[outs_in] * len(outs),
        scratch_shapes=scratch,
        compiler_params=pltpu.CompilerParams(vmem_limit_bytes=24 * 2**20),
        cost_estimate=pl.CostEstimate(flops=flops, bytes_accessed=moved, transcendentals=0),
    )(*arrays)


def index_bits():
    return lax.axis_size(AXIS).bit_length() - 1


def transposed_dot(basis, vec):
    return lax.dot_general(basis, vec, (((0,), (0,)), ((), ())), preferred_element_type=F32)


def parity_of():
    return lax.axis_index(AXIS) % 2


def own_level(slot):
    return 1 - parity_of() + 2 * slot


def other_level(slot):
    return parity_of() + 2 * slot


def first_kernel(bases_in, vec_in, out_ref, bases_ref, vec_ref, sems):
    rank = bases_in.shape[2]

    def basis_copy(level, sem):
        return pltpu.make_async_copy(bases_in.at[level], bases_ref.at[level], sem)

    copies = [pltpu.make_async_copy(vec_in, vec_ref, sems.at[0])]
    copies += [basis_copy(other_level(slot), sems.at[1 + slot]) for slot in range(2)]
    later = [basis_copy(own_level(slot), sems.at[3 + slot]) for slot in range(2)]
    for copy in copies + later:
        copy.start()
    for copy in copies:
        copy.wait()
    basis = jnp.concatenate([bases_ref[other_level(slot)] for slot in range(2)], axis=1)
    proj = transposed_dot(basis, vec_ref[...])
    out_ref[0] = proj[:rank]
    out_ref[1] = proj[rank:]
    for copy in later:
        copy.wait()


def kept_kernel(bases_ref, vec_ref, high_ref, low_ref):
    rank = bases_ref.shape[2]
    both = jnp.concatenate([bases_ref[own_level(slot)] for slot in range(2)], axis=1)
    proj = transposed_dot(both, vec_ref[...])
    high_ref[...] = proj[:rank]
    low_ref[...] = proj[rank:]


def prepare_kernel(couplings_ref, bases_ref, oriented_ref, turned_ref):
    myself = lax.axis_index(AXIS)
    bits = index_bits()
    rank = bases_ref.shape[2]
    for level in range(bases_ref.shape[0]):
        coupling = couplings_ref[(1 << level) - 1 + (myself >> bits - level)].astype(F32)
        side = myself >> bits - level - 1 & 1
        oriented_ref[level] = jnp.where(side == 0, coupling, coupling.T).astype(BF16)
    for slot in range(2):
        turned_ref[pl.ds(slot * rank, rank), :] = bases_ref[other_level(slot)].T
        turned_ref[pl.ds((2 + slot) * rank, rank), :] = bases_ref[own_level(slot)].T


def weighted(weights_ref, values, rows):
    columns = weights_ref[...].T
    blocks = range(rows.start // SPAN, rows.stop // SPAN)
    column = jnp.concatenate([columns[:, block : block + 1] for block in blocks], axis=0)
    return (column * values).astype(BF16)


def base_kernel(leaves_ref, vec_ref, weights_ref, turned_ref, part_ref, base_ref):
    total = None
    for leaf in range(vec_ref.shape[0] // LEAF):
        rows = slice(leaf * LEAF, (leaf + 1) * LEAF)
        near = jnp.dot(leaves_ref[rows, :], vec_ref[rows, :], preferred_element_type=F32)
        part_ref[rows, :] = near
        term = jnp.dot(turned_ref[:, rows], weighted(weights_ref, near, rows), preferred_element_type=F32)
        total = term if total is None else total + term
    base_ref[...] = total


def gram_kernel(bases_ref, weights_ref, turned_ref, keep_ref, send_ref):
    rank, rows_dev = bases_ref.shape[2], bases_ref.shape[1]
    total = None
    for chunk in range(rows_dev // CHUNK):
        rows = slice(chunk * CHUNK, (chunk + 1) * CHUNK)
        order = [other_level(slot) for slot in range(2)] + [own_level(slot) for slot in range(2)]
        basis = jnp.concatenate([bases_ref[level, rows, :] for level in order], axis=1)
        basis = weighted(weights_ref, basis.astype(F32), rows)
        term = jnp.dot(turned_ref[:, rows], basis, preferred_element_type=F32)
        total = term if total is None else total + term
    keep_ref[...] = total[:, 2 * rank :]
    send_ref[: 2 * rank, :] = total[2 * rank :, : 2 * rank]
    send_ref[2 * rank :, :] = total[: 2 * rank, : 2 * rank]


def coefficients(oriented_ref, level, factor, sums):
    quotient = (sums * factor).astype(BF16)
    return jnp.dot(oriented_ref[level], quotient, preferred_element_type=F32).astype(BF16)


def own_coefficients(oriented_ref, slot, sums, factors):
    factor = jnp.where(parity_of() == 1, factors[2 * slot], factors[2 * slot + 1])
    return coefficients(oriented_ref, own_level(slot), factor, sums)


def other_coefficients(oriented_ref, slot, sums, factors):
    factor = jnp.where(parity_of() == 1, factors[2 * slot + 1], factors[2 * slot])
    return coefficients(oriented_ref, other_level(slot), factor, sums)


def low_kernel(factors, oriented_ref, low_ref, keep_ref, got_ref, base_ref, sums_ref, gram_ref):
    gram = keep_ref[...] + got_ref[...]
    rough = gram.astype(BF16)
    rest = (gram - rough.astype(F32)).astype(BF16)
    rank = low_ref.shape[0]
    both = jnp.concatenate([rough[:, rank:], rest[:, rank:]], axis=1)
    coeffs = own_coefficients(oriented_ref, 1, low_ref[...], factors)
    delta = jnp.dot(both, jnp.concatenate([coeffs] * 2, axis=0), preferred_element_type=F32)
    sums_ref[...] = base_ref[...] + delta
    gram_ref[:, :rank] = rough[:, :rank]
    gram_ref[:, rank:] = rest[:, :rank]


def middle_kernel(factors, oriented_ref, high_ref, gram_ref, sums_ref, send_ref, keep_high_ref, keep_low_ref):
    coeffs = own_coefficients(oriented_ref, 0, high_ref[...], factors)
    delta = jnp.dot(gram_ref[...], jnp.concatenate([coeffs] * 2, axis=0), preferred_element_type=F32)
    proj = sums_ref[...] + delta
    rank = high_ref.shape[0]
    send_ref[0] = proj[:rank]
    send_ref[1] = proj[rank : 2 * rank]
    keep_high_ref[...] = proj[2 * rank : 3 * rank]
    keep_low_ref[...] = proj[3 * rank :]


def second_part_kernel(
    factors, oriented_ref, high_ref, low_ref, high_other_ref, low_other_ref, bases_ref, part_ref, weights_ref, leaves_ref, out_ref, buf
):
    pieces = []
    order = []
    for slot, (own_ref, other_ref) in enumerate(((high_ref, high_other_ref), (low_ref, low_other_ref))):
        pieces += [own_coefficients(oriented_ref, slot, own_ref[...], factors)]
        pieces += [other_coefficients(oriented_ref, slot, other_ref[...], factors)]
        order += [own_level(slot), other_level(slot)]
    coeffs = jnp.concatenate(pieces, axis=0)
    for leaf in range(part_ref.shape[0] // LEAF):
        rows = slice(leaf * LEAF, (leaf + 1) * LEAF)
        basis = jnp.concatenate([bases_ref[level, rows, :] for level in order], axis=1)
        first = part_ref[rows, :] + jnp.dot(basis, coeffs, preferred_element_type=F32)
        buf[rows, :] = weighted(weights_ref, first, rows)
        out_ref[rows, :] = jnp.dot(leaves_ref[rows, :], buf[rows, :], preferred_element_type=F32)


def near_result_kernel(factors, oriented_ref, high_ref, low_ref, other_ref, bases_ref, part_ref, out_ref):
    pieces = [
        own_coefficients(oriented_ref, 0, high_ref[...], factors),
        own_coefficients(oriented_ref, 1, low_ref[...], factors),
        other_coefficients(oriented_ref, 1, other_ref[...], factors),
    ]
    order = [own_level(0), own_level(1), other_level(1)]
    basis = jnp.concatenate([bases_ref[level] for level in order], axis=1)
    coeffs = jnp.concatenate(pieces, axis=0)
    out_ref[...] = part_ref[...] + jnp.dot(basis, coeffs, preferred_element_type=F32)


def result_kernel(factors, oriented_ref, other_ref, bases_ref, part_ref, result_ref, buf, sems):
    coeffs = other_coefficients(oriented_ref, 0, other_ref[...], factors)
    copies = []
    for chunk in range(part_ref.shape[0] // CHUNK):
        rows = pl.ds(chunk * CHUNK, CHUNK)
        basis = bases_ref[other_level(0), rows, :]
        total = part_ref[rows, :] + jnp.dot(basis, coeffs, preferred_element_type=F32)
        buf[rows, :] = total.astype(BF16)
        copies.append(pltpu.make_async_copy(buf.at[rows, :], result_ref.at[rows, :], sems.at[chunk]))
        copies[-1].start()
    for copy in copies:
        copy.wait()


def on_device(signal, leaves, bases, couplings, weights):
    count = lax.axis_size(AXIS)
    bits = index_bits()
    rows_dev, width = signal.shape
    levels, _, rank = bases.shape
    odd = parity_of() == 1
    far1, far2, far3, far4 = (1 << (bits - level - 1) for level in range(levels))
    factors = [1.0 / math.sqrt(rows_dev * (count >> level + 1) * rank) for level in range(levels)]
    weight_rows = weights.reshape(rows_dev // SPAN, SPAN)
    mults = rows_dev * width * rank * 2
    chunks = rows_dev // CHUNK
    sums_shape = jax.ShapeDtypeStruct((rank, width), F32)
    pair_shape = jax.ShapeDtypeStruct((2, rank, width), F32)
    part_shape = jax.ShapeDtypeStruct((rows_dev, width), F32)
    gram_shape = jax.ShapeDtypeStruct((levels * rank, 2 * rank), F32)

    def swap(value, odd_mask, even_mask):
        pairs = [(source, source ^ (odd_mask if source % 2 else even_mask)) for source in range(count)]
        return lax.ppermute(value, AXIS, pairs)

    def beside(arrays, *riders):
        return lax.optimization_barrier((*arrays, *riders))

    def begin(send, high, low):
        got = swap(send, 1, 1)
        high = high + got[0]
        low = low + got[1]
        for bit in range(1, bits - levels):
            high = high + swap(high, 1 << bit, 1 << bit)
            low = low + swap(low, 1 << bit, 1 << bit)
        return high, low

    def rounds(high, low, rider_one, rider_two, rider_three, passenger=None):
        near = swap(high, far1, far4)
        across = swap(high, far1 | far2, far3)
        near, across, *ridden = beside((near, across), *rider_one())
        high = jnp.where(odd, near + across, high + near)
        got = swap(high, far3, far2)
        low, passenger = beside((swap(low, far3, far4),), ridden.pop() if passenger is None else passenger)
        passenger = swap(passenger, 1, 1)
        got, *ridden = beside((got,), *rider_two(*ridden))
        high = jnp.where(odd, high + got, got)
        low = jnp.where(odd, low + swap(low, far4, far4), low)
        got = swap(high, far4, far3)
        got, *ridden = beside((got,), *rider_three(low, passenger, *ridden))
        return high + got, low, *ridden

    send, bases, signal = call(
        first_kernel,
        [pair_shape, jax.ShapeDtypeStruct(bases.shape, BF16), jax.ShapeDtypeStruct(signal.shape, BF16)],
        [pltpu.with_memory_space_constraint(array, pltpu.HBM) for array in (bases, signal)],
        2 * mults,
        arrays_in=HBM,
        scratch=[pltpu.SemaphoreType.DMA((5,))],
    )
    kept = call(kept_kernel, [sums_shape] * 2, [bases, signal], 2 * mults)

    def first_riders():
        oriented, turned = call(
            prepare_kernel,
            [
                jax.ShapeDtypeStruct((levels, rank, rank), BF16),
                jax.ShapeDtypeStruct((levels * rank, rows_dev), BF16),
            ],
            [couplings, bases],
            mults,
        )
        keep, send = call(gram_kernel, [gram_shape] * 2, [bases, weight_rows, turned], 2 * levels * mults)
        return oriented, turned, keep, send

    def second_riders(oriented, turned, keep):
        part, base = call(
            base_kernel,
            [part_shape, jax.ShapeDtypeStruct((levels * rank, width), F32)],
            [leaves, signal, weight_rows, turned],
            (LEAF // rank + levels) * mults,
        )
        return oriented, keep, part, base

    def third_riders(low, got, oriented, keep, part, base):
        sums, gram = call(
            functools.partial(low_kernel, factors),
            [
                jax.ShapeDtypeStruct((levels * rank, width), F32),
                jax.ShapeDtypeStruct((levels * rank, 2 * rank), BF16),
            ],
            [oriented, low, keep, got, base],
            mults,
        )
        return oriented, part, sums, gram

    high, low, oriented, part, sums, gram = rounds(
        *begin(send, *kept), first_riders, second_riders, third_riders
    )
    high, low_other = beside((high, swap(low, 1, 1)))
    send, *kept = call(
        functools.partial(middle_kernel, factors),
        [pair_shape, sums_shape, sums_shape],
        [oriented, high, gram, sums],
        mults,
    )
    next_high, next_low, high, low = beside(begin(send, *kept), high, low)

    def second_part(_, high_other):
        return call(
            functools.partial(second_part_kernel, factors),
            [part_shape],
            [oriented, high, low, high_other, low_other, bases, part, weight_rows, leaves],
            (LEAF // rank + levels) * mults,
            scratch=[pltpu.VMEM((rows_dev, width), BF16)],
        )

    high, low, part = rounds(next_high, next_low, tuple, tuple, second_part, high)
    low_other, high_other = swap(low, 1, 1), swap(high, 1, 1)
    (part,) = call(
        functools.partial(near_result_kernel, factors),
        [part_shape],
        [oriented, high, low, low_other, bases, part],
        3 * mults,
    )
    (result,) = call(
        functools.partial(result_kernel, factors),
        [jax.ShapeDtypeStruct((rows_dev, width), BF16)],
        [oriented, high_other, bases, part],
        mults,
        outs_in=HBM,
        scratch=[pltpu.VMEM((rows_dev, width), BF16), pltpu.SemaphoreType.DMA((chunks,))],
    )
    return result


def solution(mesh):
    in_specs = (P("rows", None), P("rows", None), P(None, "rows", None), P(), P("rows"))
    out_specs = P("rows", None)
    return jax.shard_map(
        on_device, mesh=mesh, in_specs=in_specs, out_specs=out_specs, check_vma=False
    )
```

```python
import functools
import math

import jax
import jax.numpy as jnp
from jax import lax
from jax.experimental import pallas as pl
from jax.experimental.pallas import tpu as pltpu
from jax.sharding import PartitionSpec as P

AXIS = "rows"
LEAF = 512
CHUNK = 256
SPAN = 128
F32 = jnp.float32
BF16 = jnp.bfloat16


VMEM = pl.BlockSpec(memory_space=pltpu.VMEM)
HBM = pl.BlockSpec(memory_space=pltpu.HBM)


def call(kernel, outs, arrays, flops, arrays_in=VMEM, outs_in=VMEM, scratch=()):
    moved = sum(math.prod(a.shape) * a.dtype.itemsize for a in (*arrays, *outs))
    return pl.pallas_call(
        kernel,
        out_shape=outs,
        in_specs=[arrays_in] * len(arrays),
        out_specs=[outs_in] * len(outs),
        scratch_shapes=scratch,
        compiler_params=pltpu.CompilerParams(vmem_limit_bytes=24 * 2**20),
        cost_estimate=pl.CostEstimate(flops=flops, bytes_accessed=moved, transcendentals=0),
    )(*arrays)


def index_bits():
    return lax.axis_size(AXIS).bit_length() - 1


def transposed_dot(basis, vec):
    return lax.dot_general(basis, vec, (((0,), (0,)), ((), ())), preferred_element_type=F32)


def parity_of():
    return lax.axis_index(AXIS) % 2


def own_level(slot):
    return 1 - parity_of() + 2 * slot


def other_level(slot):
    return parity_of() + 2 * slot


def first_kernel(bases_in, vec_in, out_ref, bases_ref, vec_ref, sems):
    rank = bases_in.shape[2]

    def basis_copy(level, sem):
        return pltpu.make_async_copy(bases_in.at[level], bases_ref.at[level], sem)

    copies = [pltpu.make_async_copy(vec_in, vec_ref, sems.at[0])]
    copies += [basis_copy(other_level(slot), sems.at[1 + slot]) for slot in range(2)]
    later = [basis_copy(own_level(slot), sems.at[3 + slot]) for slot in range(2)]
    for copy in copies + later:
        copy.start()
    for copy in copies:
        copy.wait()
    basis = jnp.concatenate([bases_ref[other_level(slot)] for slot in range(2)], axis=1)
    proj = transposed_dot(basis, vec_ref[...])
    out_ref[0] = proj[:rank]
    out_ref[1] = proj[rank:]
    for copy in later:
        copy.wait()


def kept_kernel(bases_ref, vec_ref, high_ref, low_ref):
    rank = bases_ref.shape[2]
    both = jnp.concatenate([bases_ref[own_level(slot)] for slot in range(2)], axis=1)
    proj = transposed_dot(both, vec_ref[...])
    high_ref[...] = proj[:rank]
    low_ref[...] = proj[rank:]


def prepare_kernel(couplings_ref, bases_ref, oriented_ref, turned_ref):
    myself = lax.axis_index(AXIS)
    bits = index_bits()
    rank = bases_ref.shape[2]
    for level in range(bases_ref.shape[0]):
        coupling = couplings_ref[(1 << level) - 1 + (myself >> bits - level)].astype(F32)
        side = myself >> bits - level - 1 & 1
        oriented_ref[level] = jnp.where(side == 0, coupling, coupling.T).astype(BF16)
    for slot in range(2):
        turned_ref[pl.ds(slot * rank, rank), :] = bases_ref[other_level(slot)].T
        turned_ref[pl.ds((2 + slot) * rank, rank), :] = bases_ref[own_level(slot)].T


def weighted(weights_ref, values, rows):
    columns = weights_ref[...].T
    blocks = range(rows.start // SPAN, rows.stop // SPAN)
    column = jnp.concatenate([columns[:, block : block + 1] for block in blocks], axis=0)
    return (column * values).astype(BF16)


def near_kernel(leaves_ref, vec_ref, part_ref):
    for leaf in range(vec_ref.shape[0] // LEAF):
        rows = slice(leaf * LEAF, (leaf + 1) * LEAF)
        part_ref[rows, :] = jnp.dot(leaves_ref[rows, :], vec_ref[rows, :], preferred_element_type=F32)


def gram_kernel(bases_ref, weights_ref, turned_ref, keep_ref, send_ref):
    rank, rows_dev = bases_ref.shape[2], bases_ref.shape[1]
    total = None
    for chunk in range(rows_dev // CHUNK):
        rows = slice(chunk * CHUNK, (chunk + 1) * CHUNK)
        order = [other_level(slot) for slot in range(2)] + [own_level(slot) for slot in range(2)]
        basis = jnp.concatenate([bases_ref[level, rows, :] for level in order], axis=1)
        basis = weighted(weights_ref, basis.astype(F32), rows)
        term = jnp.dot(turned_ref[:, rows], basis, preferred_element_type=F32)
        total = term if total is None else total + term
    keep_ref[...] = total[:, 2 * rank :]
    send_ref[: 2 * rank, :] = total[2 * rank :, : 2 * rank]
    send_ref[2 * rank :, :] = total[: 2 * rank, : 2 * rank]


def coefficients(oriented_ref, level, factor, sums):
    quotient = (sums * factor).astype(BF16)
    return jnp.dot(oriented_ref[level], quotient, preferred_element_type=F32).astype(BF16)


def own_coefficients(oriented_ref, slot, sums, factors):
    factor = jnp.where(parity_of() == 1, factors[2 * slot], factors[2 * slot + 1])
    return coefficients(oriented_ref, own_level(slot), factor, sums)


def other_coefficients(oriented_ref, slot, sums, factors):
    factor = jnp.where(parity_of() == 1, factors[2 * slot + 1], factors[2 * slot])
    return coefficients(oriented_ref, other_level(slot), factor, sums)


def low_kernel(
    factors, oriented_ref, low_ref, keep_ref, got_ref, part_ref, weights_ref, turned_ref, sums_ref, gram_ref
):
    gram = keep_ref[...] + got_ref[...]
    rough = gram.astype(BF16)
    rest = (gram - rough.astype(F32)).astype(BF16)
    rank = low_ref.shape[0]
    both = jnp.concatenate([rough[:, rank:], rest[:, rank:]], axis=1)
    coeffs = own_coefficients(oriented_ref, 1, low_ref[...], factors)
    total = jnp.dot(both, jnp.concatenate([coeffs] * 2, axis=0), preferred_element_type=F32)
    for leaf in range(part_ref.shape[0] // LEAF):
        rows = slice(leaf * LEAF, (leaf + 1) * LEAF)
        near = weighted(weights_ref, part_ref[rows, :], rows)
        total = total + jnp.dot(turned_ref[:, rows], near, preferred_element_type=F32)
    sums_ref[...] = total
    gram_ref[:, :rank] = rough[:, :rank]
    gram_ref[:, rank:] = rest[:, :rank]


def middle_kernel(factors, oriented_ref, high_ref, gram_ref, sums_ref, send_ref, keep_high_ref, keep_low_ref):
    coeffs = own_coefficients(oriented_ref, 0, high_ref[...], factors)
    delta = jnp.dot(gram_ref[...], jnp.concatenate([coeffs] * 2, axis=0), preferred_element_type=F32)
    proj = sums_ref[...] + delta
    rank = high_ref.shape[0]
    send_ref[0] = proj[:rank]
    send_ref[1] = proj[rank : 2 * rank]
    keep_high_ref[...] = proj[2 * rank : 3 * rank]
    keep_low_ref[...] = proj[3 * rank :]


def second_part_kernel(
    factors, oriented_ref, high_ref, low_ref, high_other_ref, low_other_ref, bases_ref, part_ref, weights_ref, leaves_ref, out_ref, buf
):
    pieces = []
    order = []
    for slot, (own_ref, other_ref) in enumerate(((high_ref, high_other_ref), (low_ref, low_other_ref))):
        pieces += [own_coefficients(oriented_ref, slot, own_ref[...], factors)]
        pieces += [other_coefficients(oriented_ref, slot, other_ref[...], factors)]
        order += [own_level(slot), other_level(slot)]
    coeffs = jnp.concatenate(pieces, axis=0)
    for leaf in range(part_ref.shape[0] // LEAF):
        rows = slice(leaf * LEAF, (leaf + 1) * LEAF)
        basis = jnp.concatenate([bases_ref[level, rows, :] for level in order], axis=1)
        first = part_ref[rows, :] + jnp.dot(basis, coeffs, preferred_element_type=F32)
        buf[rows, :] = weighted(weights_ref, first, rows)
        out_ref[rows, :] = jnp.dot(leaves_ref[rows, :], buf[rows, :], preferred_element_type=F32)


def near_result_kernel(factors, oriented_ref, high_ref, low_ref, other_ref, bases_ref, part_ref, out_ref):
    pieces = [
        own_coefficients(oriented_ref, 0, high_ref[...], factors),
        own_coefficients(oriented_ref, 1, low_ref[...], factors),
        other_coefficients(oriented_ref, 1, other_ref[...], factors),
    ]
    order = [own_level(0), own_level(1), other_level(1)]
    basis = jnp.concatenate([bases_ref[level] for level in order], axis=1)
    coeffs = jnp.concatenate(pieces, axis=0)
    out_ref[...] = part_ref[...] + jnp.dot(basis, coeffs, preferred_element_type=F32)


def result_kernel(factors, oriented_ref, other_ref, bases_ref, part_ref, result_ref, buf, sems):
    coeffs = other_coefficients(oriented_ref, 0, other_ref[...], factors)
    copies = []
    for chunk in range(part_ref.shape[0] // CHUNK):
        rows = pl.ds(chunk * CHUNK, CHUNK)
        basis = bases_ref[other_level(0), rows, :]
        total = part_ref[rows, :] + jnp.dot(basis, coeffs, preferred_element_type=F32)
        buf[rows, :] = total.astype(BF16)
        copies.append(pltpu.make_async_copy(buf.at[rows, :], result_ref.at[rows, :], sems.at[chunk]))
        copies[-1].start()
    for copy in copies:
        copy.wait()


def on_device(signal, leaves, bases, couplings, weights):
    count = lax.axis_size(AXIS)
    bits = index_bits()
    rows_dev, width = signal.shape
    levels, _, rank = bases.shape
    odd = parity_of() == 1
    far1, far2, far3, far4 = (1 << (bits - level - 1) for level in range(levels))
    factors = [1.0 / math.sqrt(rows_dev * (count >> level + 1) * rank) for level in range(levels)]
    weight_rows = weights.reshape(rows_dev // SPAN, SPAN)
    mults = rows_dev * width * rank * 2
    chunks = rows_dev // CHUNK
    sums_shape = jax.ShapeDtypeStruct((rank, width), F32)
    pair_shape = jax.ShapeDtypeStruct((2, rank, width), F32)
    part_shape = jax.ShapeDtypeStruct((rows_dev, width), F32)
    gram_shape = jax.ShapeDtypeStruct((levels * rank, 2 * rank), F32)

    def swap(value, odd_mask, even_mask):
        pairs = [(source, source ^ (odd_mask if source % 2 else even_mask)) for source in range(count)]
        return lax.ppermute(value, AXIS, pairs)

    def beside(arrays, *riders):
        return lax.optimization_barrier((*arrays, *riders))

    def begin(send, high, low):
        got = swap(send, 1, 1)
        high = high + got[0]
        low = low + got[1]
        for bit in range(1, bits - levels):
            high = high + swap(high, 1 << bit, 1 << bit)
            low = low + swap(low, 1 << bit, 1 << bit)
        return high, low

    def rounds(high, low, rider_one, rider_two, rider_three, passenger=None):
        near = swap(high, far1, far4)
        across = swap(high, far1 | far2, far3)
        near, across, *ridden = beside((near, across), *rider_one())
        high = jnp.where(odd, near + across, high + near)
        got = swap(high, far3, far2)
        low, passenger = beside((swap(low, far3, far4),), ridden.pop() if passenger is None else passenger)
        passenger = swap(passenger, 1, 1)
        got, *ridden = beside((got,), *rider_two(*ridden))
        high = jnp.where(odd, high + got, got)
        low = jnp.where(odd, low + swap(low, far4, far2), low)
        got = swap(high, far4, far3)
        got, *ridden = beside((got,), *rider_three(low, passenger, *ridden))
        return high + got, low, *ridden

    send, bases, signal = call(
        first_kernel,
        [pair_shape, jax.ShapeDtypeStruct(bases.shape, BF16), jax.ShapeDtypeStruct(signal.shape, BF16)],
        [pltpu.with_memory_space_constraint(array, pltpu.HBM) for array in (bases, signal)],
        2 * mults,
        arrays_in=HBM,
        scratch=[pltpu.SemaphoreType.DMA((5,))],
    )
    kept = call(kept_kernel, [sums_shape] * 2, [bases, signal], 2 * mults)

    def first_riders():
        oriented, turned = call(
            prepare_kernel,
            [
                jax.ShapeDtypeStruct((levels, rank, rank), BF16),
                jax.ShapeDtypeStruct((levels * rank, rows_dev), BF16),
            ],
            [couplings, bases],
            mults,
        )
        keep, send = call(gram_kernel, [gram_shape] * 2, [bases, weight_rows, turned], 2 * levels * mults)
        return oriented, turned, keep, send

    def second_riders(oriented, turned, keep):
        (part,) = call(near_kernel, [part_shape], [leaves, signal], LEAF // rank * mults)
        return oriented, turned, keep, part

    def third_riders(low, got, oriented, turned, keep, part):
        sums, gram = call(
            functools.partial(low_kernel, factors),
            [
                jax.ShapeDtypeStruct((levels * rank, width), F32),
                jax.ShapeDtypeStruct((levels * rank, 2 * rank), BF16),
            ],
            [oriented, low, keep, got, part, weight_rows, turned],
            (1 + levels) * mults,
        )
        return oriented, part, sums, gram

    high, low, oriented, part, sums, gram = rounds(
        *begin(send, *kept), first_riders, second_riders, third_riders
    )
    high, low_other = beside((high, swap(low, 1, 1)))
    send, *kept = call(
        functools.partial(middle_kernel, factors),
        [pair_shape, sums_shape, sums_shape],
        [oriented, high, gram, sums],
        mults,
    )
    next_high, next_low, high, low = beside(begin(send, *kept), high, low)

    def second_part(_, high_other):
        return call(
            functools.partial(second_part_kernel, factors),
            [part_shape],
            [oriented, high, low, high_other, low_other, bases, part, weight_rows, leaves],
            (LEAF // rank + levels) * mults,
            scratch=[pltpu.VMEM((rows_dev, width), BF16)],
        )

    high, low, part = rounds(next_high, next_low, tuple, tuple, second_part, high)
    low_other, high_other = swap(low, 1, 1), swap(high, 1, 1)
    (part,) = call(
        functools.partial(near_result_kernel, factors),
        [part_shape],
        [oriented, high, low, low_other, bases, part],
        3 * mults,
    )
    (result,) = call(
        functools.partial(result_kernel, factors),
        [jax.ShapeDtypeStruct((rows_dev, width), BF16)],
        [oriented, high_other, bases, part],
        mults,
        outs_in=HBM,
        scratch=[pltpu.VMEM((rows_dev, width), BF16), pltpu.SemaphoreType.DMA((chunks,))],
    )
    return result


def solution(mesh):
    in_specs = (P("rows", None), P("rows", None), P(None, "rows", None), P(), P("rows"))
    out_specs = P("rows", None)
    return jax.shard_map(
        on_device, mesh=mesh, in_specs=in_specs, out_specs=out_specs, check_vma=False
    )
```

```python
import functools
import math

import jax
import jax.numpy as jnp
from jax import lax
from jax.experimental import pallas as pl
from jax.experimental.pallas import tpu as pltpu
from jax.sharding import PartitionSpec as P

AXIS = "rows"
LEAF = 512
CHUNK = 256
SPAN = 128
F32 = jnp.float32
BF16 = jnp.bfloat16


VMEM = pl.BlockSpec(memory_space=pltpu.VMEM)
HBM = pl.BlockSpec(memory_space=pltpu.HBM)


def call(kernel, outs, arrays, flops, arrays_in=VMEM, outs_in=VMEM, scratch=()):
    moved = sum(math.prod(a.shape) * a.dtype.itemsize for a in (*arrays, *outs))
    return pl.pallas_call(
        kernel,
        out_shape=outs,
        in_specs=[arrays_in] * len(arrays),
        out_specs=[outs_in] * len(outs),
        scratch_shapes=scratch,
        compiler_params=pltpu.CompilerParams(vmem_limit_bytes=24 * 2**20),
        cost_estimate=pl.CostEstimate(flops=flops, bytes_accessed=moved, transcendentals=0),
    )(*arrays)


def index_bits():
    return lax.axis_size(AXIS).bit_length() - 1


def transposed_dot(basis, vec):
    return lax.dot_general(basis, vec, (((0,), (0,)), ((), ())), preferred_element_type=F32)


def parity_of():
    return lax.axis_index(AXIS) % 2


def own_level(slot):
    return 1 - parity_of() + 2 * slot


def other_level(slot):
    return parity_of() + 2 * slot


def first_kernel(bases_in, vec_in, out_ref, bases_ref, vec_ref, sems):
    rank = bases_in.shape[2]

    def basis_copy(level, sem):
        return pltpu.make_async_copy(bases_in.at[level], bases_ref.at[level], sem)

    copies = [pltpu.make_async_copy(vec_in, vec_ref, sems.at[0])]
    copies += [basis_copy(other_level(slot), sems.at[1 + slot]) for slot in range(2)]
    later = [basis_copy(own_level(slot), sems.at[3 + slot]) for slot in range(2)]
    for copy in copies + later:
        copy.start()
    for copy in copies:
        copy.wait()
    basis = jnp.concatenate([bases_ref[other_level(slot)] for slot in range(2)], axis=1)
    proj = transposed_dot(basis, vec_ref[...])
    out_ref[0] = proj[:rank]
    out_ref[1] = proj[rank:]
    for copy in later:
        copy.wait()


def kept_kernel(bases_ref, vec_ref, high_ref, low_ref):
    rank = bases_ref.shape[2]
    both = jnp.concatenate([bases_ref[own_level(slot)] for slot in range(2)], axis=1)
    proj = transposed_dot(both, vec_ref[...])
    high_ref[...] = proj[:rank]
    low_ref[...] = proj[rank:]


def prepare_kernel(couplings_ref, bases_ref, oriented_ref, turned_ref):
    myself = lax.axis_index(AXIS)
    bits = index_bits()
    rank = bases_ref.shape[2]
    for level in range(bases_ref.shape[0]):
        coupling = couplings_ref[(1 << level) - 1 + (myself >> bits - level)].astype(F32)
        side = myself >> bits - level - 1 & 1
        oriented_ref[level] = jnp.where(side == 0, coupling, coupling.T).astype(BF16)
    for slot in range(2):
        turned_ref[pl.ds(slot * rank, rank), :] = bases_ref[other_level(slot)].T
        turned_ref[pl.ds((2 + slot) * rank, rank), :] = bases_ref[own_level(slot)].T


def weighted(weights_ref, values, rows):
    columns = weights_ref[...].T
    blocks = range(rows.start // SPAN, rows.stop // SPAN)
    column = jnp.concatenate([columns[:, block : block + 1] for block in blocks], axis=0)
    return (column * values).astype(BF16)


def near_kernel(leaves_ref, vec_ref, part_ref):
    for leaf in range(vec_ref.shape[0] // LEAF):
        rows = slice(leaf * LEAF, (leaf + 1) * LEAF)
        part_ref[rows, :] = jnp.dot(leaves_ref[rows, :], vec_ref[rows, :], preferred_element_type=F32)


def gram_kernel(bases_ref, weights_ref, turned_ref, keep_ref, send_ref):
    rank, rows_dev = bases_ref.shape[2], bases_ref.shape[1]
    total = None
    for chunk in range(rows_dev // CHUNK):
        rows = slice(chunk * CHUNK, (chunk + 1) * CHUNK)
        order = [other_level(slot) for slot in range(2)] + [own_level(slot) for slot in range(2)]
        basis = jnp.concatenate([bases_ref[level, rows, :] for level in order], axis=1)
        basis = weighted(weights_ref, basis.astype(F32), rows)
        term = jnp.dot(turned_ref[:, rows], basis, preferred_element_type=F32)
        total = term if total is None else total + term
    keep_ref[...] = total[:, 2 * rank :]
    send_ref[: 2 * rank, :] = total[2 * rank :, : 2 * rank]
    send_ref[2 * rank :, :] = total[: 2 * rank, : 2 * rank]


def coefficients(oriented_ref, level, factor, sums):
    quotient = (sums * factor).astype(BF16)
    return jnp.dot(oriented_ref[level], quotient, preferred_element_type=F32).astype(BF16)


def own_coefficients(oriented_ref, slot, sums, factors):
    factor = jnp.where(parity_of() == 1, factors[2 * slot], factors[2 * slot + 1])
    return coefficients(oriented_ref, own_level(slot), factor, sums)


def other_coefficients(oriented_ref, slot, sums, factors):
    factor = jnp.where(parity_of() == 1, factors[2 * slot + 1], factors[2 * slot])
    return coefficients(oriented_ref, other_level(slot), factor, sums)


def low_kernel(
    factors, oriented_ref, low_ref, keep_ref, got_ref, part_ref, weights_ref, turned_ref, sums_ref, gram_ref
):
    gram = keep_ref[...] + got_ref[...]
    rough = gram.astype(BF16)
    rest = (gram - rough.astype(F32)).astype(BF16)
    rank = low_ref.shape[0]
    both = jnp.concatenate([rough[:, rank:], rest[:, rank:]], axis=1)
    coeffs = own_coefficients(oriented_ref, 1, low_ref[...], factors)
    total = jnp.dot(both, jnp.concatenate([coeffs] * 2, axis=0), preferred_element_type=F32)
    for leaf in range(part_ref.shape[0] // LEAF):
        rows = slice(leaf * LEAF, (leaf + 1) * LEAF)
        near = weighted(weights_ref, part_ref[rows, :], rows)
        total = total + jnp.dot(turned_ref[:, rows], near, preferred_element_type=F32)
    sums_ref[...] = total
    gram_ref[:, :rank] = rough[:, :rank]
    gram_ref[:, rank:] = rest[:, :rank]


def middle_kernel(factors, oriented_ref, high_ref, gram_ref, sums_ref, send_ref, keep_high_ref, keep_low_ref):
    coeffs = own_coefficients(oriented_ref, 0, high_ref[...], factors)
    delta = jnp.dot(gram_ref[...], jnp.concatenate([coeffs] * 2, axis=0), preferred_element_type=F32)
    proj = sums_ref[...] + delta
    rank = high_ref.shape[0]
    send_ref[0] = proj[:rank]
    send_ref[1] = proj[rank : 2 * rank]
    keep_high_ref[...] = proj[2 * rank : 3 * rank]
    keep_low_ref[...] = proj[3 * rank :]


def second_part_kernel(
    factors, oriented_ref, high_ref, low_ref, high_other_ref, low_other_ref, bases_ref, part_ref, weights_ref, leaves_ref, out_ref, buf
):
    pieces = []
    order = []
    for slot, (own_ref, other_ref) in enumerate(((high_ref, high_other_ref), (low_ref, low_other_ref))):
        pieces += [own_coefficients(oriented_ref, slot, own_ref[...], factors)]
        pieces += [other_coefficients(oriented_ref, slot, other_ref[...], factors)]
        order += [own_level(slot), other_level(slot)]
    coeffs = jnp.concatenate(pieces, axis=0)
    for leaf in range(part_ref.shape[0] // LEAF):
        rows = slice(leaf * LEAF, (leaf + 1) * LEAF)
        basis = jnp.concatenate([bases_ref[level, rows, :] for level in order], axis=1)
        first = part_ref[rows, :] + jnp.dot(basis, coeffs, preferred_element_type=F32)
        buf[rows, :] = weighted(weights_ref, first, rows)
        out_ref[rows, :] = jnp.dot(leaves_ref[rows, :], buf[rows, :], preferred_element_type=F32)


def near_result_kernel(factors, oriented_ref, high_ref, low_ref, other_ref, bases_ref, part_ref, out_ref):
    pieces = [
        own_coefficients(oriented_ref, 0, high_ref[...], factors),
        own_coefficients(oriented_ref, 1, low_ref[...], factors),
        other_coefficients(oriented_ref, 1, other_ref[...], factors),
    ]
    order = [own_level(0), own_level(1), other_level(1)]
    basis = jnp.concatenate([bases_ref[level] for level in order], axis=1)
    coeffs = jnp.concatenate(pieces, axis=0)
    out_ref[...] = part_ref[...] + jnp.dot(basis, coeffs, preferred_element_type=F32)


def result_kernel(factors, oriented_ref, other_ref, bases_ref, part_ref, result_ref, buf, sems):
    coeffs = other_coefficients(oriented_ref, 0, other_ref[...], factors)
    copies = []
    for chunk in range(part_ref.shape[0] // CHUNK):
        rows = pl.ds(chunk * CHUNK, CHUNK)
        basis = bases_ref[other_level(0), rows, :]
        total = part_ref[rows, :] + jnp.dot(basis, coeffs, preferred_element_type=F32)
        buf[rows, :] = total.astype(BF16)
        copies.append(pltpu.make_async_copy(buf.at[rows, :], result_ref.at[rows, :], sems.at[chunk]))
        copies[-1].start()
    for copy in copies:
        copy.wait()


def on_device(signal, leaves, bases, couplings, weights):
    count = lax.axis_size(AXIS)
    bits = index_bits()
    rows_dev, width = signal.shape
    levels, _, rank = bases.shape
    odd = parity_of() == 1
    far1, far2, far3, far4 = (1 << (bits - level - 1) for level in range(levels))
    factors = [1.0 / math.sqrt(rows_dev * (count >> level + 1) * rank) for level in range(levels)]
    weight_rows = weights.reshape(rows_dev // SPAN, SPAN)
    mults = rows_dev * width * rank * 2
    chunks = rows_dev // CHUNK
    sums_shape = jax.ShapeDtypeStruct((rank, width), F32)
    pair_shape = jax.ShapeDtypeStruct((2, rank, width), F32)
    part_shape = jax.ShapeDtypeStruct((rows_dev, width), F32)
    gram_shape = jax.ShapeDtypeStruct((levels * rank, 2 * rank), F32)

    def swap(value, odd_mask, even_mask):
        pairs = [(source, source ^ (odd_mask if source % 2 else even_mask)) for source in range(count)]
        return lax.ppermute(value, AXIS, pairs)

    def beside(arrays, *riders):
        return lax.optimization_barrier((*arrays, *riders))

    def begin(send, high, low):
        got = swap(send, 1, 1)
        high = high + got[0]
        low = low + got[1]
        for bit in range(1, bits - levels):
            high = high + swap(high, 1 << bit, 1 << bit)
            low = low + swap(low, 1 << bit, 1 << bit)
        return high, low

    def rounds(high, low, rider_one, rider_two, rider_three, passenger=None):
        near = swap(high, far1, far4)
        across = swap(high, far1 | far2, far4)
        near, across, *ridden = beside((near, across), *rider_one())
        high = jnp.where(odd, near + across, high + near)
        got = swap(high, far3, far2)
        low, passenger = beside((swap(low, far3, far4),), ridden.pop() if passenger is None else passenger)
        passenger = swap(passenger, 1, 1)
        got, *ridden = beside((got,), *rider_two(*ridden))
        high = jnp.where(odd, high + got, got)
        low = jnp.where(odd, low + swap(low, far4, far2), low)
        got = swap(high, far4, far3)
        got, *ridden = beside((got,), *rider_three(low, passenger, *ridden))
        return high + got, low, *ridden

    send, bases, signal = call(
        first_kernel,
        [pair_shape, jax.ShapeDtypeStruct(bases.shape, BF16), jax.ShapeDtypeStruct(signal.shape, BF16)],
        [pltpu.with_memory_space_constraint(array, pltpu.HBM) for array in (bases, signal)],
        2 * mults,
        arrays_in=HBM,
        scratch=[pltpu.SemaphoreType.DMA((5,))],
    )
    kept = call(kept_kernel, [sums_shape] * 2, [bases, signal], 2 * mults)

    def first_riders():
        oriented, turned = call(
            prepare_kernel,
            [
                jax.ShapeDtypeStruct((levels, rank, rank), BF16),
                jax.ShapeDtypeStruct((levels * rank, rows_dev), BF16),
            ],
            [couplings, bases],
            mults,
        )
        keep, send = call(gram_kernel, [gram_shape] * 2, [bases, weight_rows, turned], 2 * levels * mults)
        return oriented, turned, keep, send

    def second_riders(oriented, turned, keep):
        (part,) = call(near_kernel, [part_shape], [leaves, signal], LEAF // rank * mults)
        return oriented, turned, keep, part

    def third_riders(low, got, oriented, turned, keep, part):
        sums, gram = call(
            functools.partial(low_kernel, factors),
            [
                jax.ShapeDtypeStruct((levels * rank, width), F32),
                jax.ShapeDtypeStruct((levels * rank, 2 * rank), BF16),
            ],
            [oriented, low, keep, got, part, weight_rows, turned],
            (1 + levels) * mults,
        )
        return oriented, part, sums, gram

    high, low, oriented, part, sums, gram = rounds(
        *begin(send, *kept), first_riders, second_riders, third_riders
    )
    high, low_other = beside((high, swap(low, 1, 1)))
    send, *kept = call(
        functools.partial(middle_kernel, factors),
        [pair_shape, sums_shape, sums_shape],
        [oriented, high, gram, sums],
        mults,
    )
    next_high, next_low, high, low = beside(begin(send, *kept), high, low)

    def second_part(_, high_other):
        return call(
            functools.partial(second_part_kernel, factors),
            [part_shape],
            [oriented, high, low, high_other, low_other, bases, part, weight_rows, leaves],
            (LEAF // rank + levels) * mults,
            scratch=[pltpu.VMEM((rows_dev, width), BF16)],
        )

    high, low, part = rounds(next_high, next_low, tuple, tuple, second_part, high)
    low_other, high_other = swap(low, 1, 1), swap(high, 1, 1)
    (part,) = call(
        functools.partial(near_result_kernel, factors),
        [part_shape],
        [oriented, high, low, low_other, bases, part],
        3 * mults,
    )
    (result,) = call(
        functools.partial(result_kernel, factors),
        [jax.ShapeDtypeStruct((rows_dev, width), BF16)],
        [oriented, high_other, bases, part],
        mults,
        outs_in=HBM,
        scratch=[pltpu.VMEM((rows_dev, width), BF16), pltpu.SemaphoreType.DMA((chunks,))],
    )
    return result


def solution(mesh):
    in_specs = (P("rows", None), P("rows", None), P(None, "rows", None), P(), P("rows"))
    out_specs = P("rows", None)
    return jax.shard_map(
        on_device, mesh=mesh, in_specs=in_specs, out_specs=out_specs, check_vma=False
    )
```

```python
import functools
import math

import jax
import jax.numpy as jnp
from jax import lax
from jax.experimental import pallas as pl
from jax.experimental.pallas import tpu as pltpu
from jax.sharding import PartitionSpec as P

AXIS = "rows"
LEAF = 512
CHUNK = 256
SPAN = 128
F32 = jnp.float32
BF16 = jnp.bfloat16


VMEM = pl.BlockSpec(memory_space=pltpu.VMEM)
HBM = pl.BlockSpec(memory_space=pltpu.HBM)


def call(kernel, outs, arrays, flops, arrays_in=VMEM, outs_in=VMEM, scratch=()):
    moved = sum(math.prod(a.shape) * a.dtype.itemsize for a in (*arrays, *outs))
    return pl.pallas_call(
        kernel,
        out_shape=outs,
        in_specs=[arrays_in] * len(arrays),
        out_specs=[outs_in] * len(outs),
        scratch_shapes=scratch,
        compiler_params=pltpu.CompilerParams(vmem_limit_bytes=24 * 2**20),
        cost_estimate=pl.CostEstimate(flops=flops, bytes_accessed=moved, transcendentals=0),
    )(*arrays)


def index_bits():
    return lax.axis_size(AXIS).bit_length() - 1


def transposed_dot(basis, vec):
    return lax.dot_general(basis, vec, (((0,), (0,)), ((), ())), preferred_element_type=F32)


def parity_of():
    return lax.axis_index(AXIS) % 2


def own_level(slot):
    return 1 - parity_of() + 2 * slot


def other_level(slot):
    return parity_of() + 2 * slot


def first_kernel(bases_in, vec_in, out_ref, bases_ref, vec_ref, sems):
    rank = bases_in.shape[2]

    def basis_copy(level, sem):
        return pltpu.make_async_copy(bases_in.at[level], bases_ref.at[level], sem)

    copies = [pltpu.make_async_copy(vec_in, vec_ref, sems.at[0])]
    copies += [basis_copy(other_level(slot), sems.at[1 + slot]) for slot in range(2)]
    later = [basis_copy(own_level(slot), sems.at[3 + slot]) for slot in range(2)]
    for copy in copies + later:
        copy.start()
    for copy in copies:
        copy.wait()
    basis = jnp.concatenate([bases_ref[other_level(slot)] for slot in range(2)], axis=1)
    proj = transposed_dot(basis, vec_ref[...])
    out_ref[0] = proj[:rank]
    out_ref[1] = proj[rank:]
    for copy in later:
        copy.wait()


def kept_kernel(bases_ref, vec_ref, high_ref, low_ref):
    rank = bases_ref.shape[2]
    both = jnp.concatenate([bases_ref[own_level(slot)] for slot in range(2)], axis=1)
    proj = transposed_dot(both, vec_ref[...])
    high_ref[...] = proj[:rank]
    low_ref[...] = proj[rank:]


def prepare_kernel(couplings_ref, bases_ref, oriented_ref, turned_ref):
    myself = lax.axis_index(AXIS)
    bits = index_bits()
    rank = bases_ref.shape[2]
    for level in range(bases_ref.shape[0]):
        coupling = couplings_ref[(1 << level) - 1 + (myself >> bits - level)].astype(F32)
        side = myself >> bits - level - 1 & 1
        oriented_ref[level] = jnp.where(side == 0, coupling, coupling.T).astype(BF16)
    for slot in range(2):
        turned_ref[pl.ds(slot * rank, rank), :] = bases_ref[other_level(slot)].T
        turned_ref[pl.ds((2 + slot) * rank, rank), :] = bases_ref[own_level(slot)].T


def weighted(weights_ref, values, rows):
    columns = weights_ref[...].T
    blocks = range(rows.start // SPAN, rows.stop // SPAN)
    column = jnp.concatenate([columns[:, block : block + 1] for block in blocks], axis=0)
    return (column * values).astype(BF16)


def near_kernel(leaves_ref, vec_ref, part_ref):
    for leaf in range(vec_ref.shape[0] // LEAF):
        rows = slice(leaf * LEAF, (leaf + 1) * LEAF)
        part_ref[rows, :] = jnp.dot(leaves_ref[rows, :], vec_ref[rows, :], preferred_element_type=F32)


def gram_kernel(bases_ref, weights_ref, turned_ref, keep_ref, send_ref):
    rank, rows_dev = bases_ref.shape[2], bases_ref.shape[1]
    total = None
    for chunk in range(rows_dev // CHUNK):
        rows = slice(chunk * CHUNK, (chunk + 1) * CHUNK)
        order = [other_level(slot) for slot in range(2)] + [own_level(slot) for slot in range(2)]
        basis = jnp.concatenate([bases_ref[level, rows, :] for level in order], axis=1)
        basis = weighted(weights_ref, basis.astype(F32), rows)
        term = jnp.dot(turned_ref[:, rows], basis, preferred_element_type=F32)
        total = term if total is None else total + term
    keep_ref[...] = total[:, 2 * rank :]
    send_ref[: 2 * rank, :] = total[2 * rank :, : 2 * rank]
    send_ref[2 * rank :, :] = total[: 2 * rank, : 2 * rank]


def coefficients(oriented_ref, level, factor, sums):
    quotient = (sums * factor).astype(BF16)
    return jnp.dot(oriented_ref[level], quotient, preferred_element_type=F32).astype(BF16)


def own_coefficients(oriented_ref, slot, sums, factors):
    factor = jnp.where(parity_of() == 1, factors[2 * slot], factors[2 * slot + 1])
    return coefficients(oriented_ref, own_level(slot), factor, sums)


def other_coefficients(oriented_ref, slot, sums, factors):
    factor = jnp.where(parity_of() == 1, factors[2 * slot + 1], factors[2 * slot])
    return coefficients(oriented_ref, other_level(slot), factor, sums)


def low_kernel(
    factors, oriented_ref, low_ref, keep_ref, got_ref, part_ref, weights_ref, turned_ref, sums_ref, gram_ref
):
    gram = keep_ref[...] + got_ref[...]
    rough = gram.astype(BF16)
    rest = (gram - rough.astype(F32)).astype(BF16)
    rank = low_ref.shape[0]
    both = jnp.concatenate([rough[:, rank:], rest[:, rank:]], axis=1)
    coeffs = own_coefficients(oriented_ref, 1, low_ref[...], factors)
    total = jnp.dot(both, jnp.concatenate([coeffs] * 2, axis=0), preferred_element_type=F32)
    for leaf in range(part_ref.shape[0] // LEAF):
        rows = slice(leaf * LEAF, (leaf + 1) * LEAF)
        near = weighted(weights_ref, part_ref[rows, :], rows)
        total = total + jnp.dot(turned_ref[:, rows], near, preferred_element_type=F32)
    sums_ref[...] = total
    gram_ref[:, :rank] = rough[:, :rank]
    gram_ref[:, rank:] = rest[:, :rank]


def middle_kernel(factors, oriented_ref, high_ref, gram_ref, sums_ref, send_ref, keep_high_ref, keep_low_ref):
    coeffs = own_coefficients(oriented_ref, 0, high_ref[...], factors)
    delta = jnp.dot(gram_ref[...], jnp.concatenate([coeffs] * 2, axis=0), preferred_element_type=F32)
    proj = sums_ref[...] + delta
    rank = high_ref.shape[0]
    send_ref[0] = proj[:rank]
    send_ref[1] = proj[rank : 2 * rank]
    keep_high_ref[...] = proj[2 * rank : 3 * rank]
    keep_low_ref[...] = proj[3 * rank :]


def second_part_kernel(
    factors, oriented_ref, high_ref, low_ref, high_other_ref, low_other_ref, bases_ref, part_ref, weights_ref, leaves_ref, out_ref, buf
):
    pieces = []
    order = []
    for slot, (own_ref, other_ref) in enumerate(((high_ref, high_other_ref), (low_ref, low_other_ref))):
        pieces += [own_coefficients(oriented_ref, slot, own_ref[...], factors)]
        pieces += [other_coefficients(oriented_ref, slot, other_ref[...], factors)]
        order += [own_level(slot), other_level(slot)]
    coeffs = jnp.concatenate(pieces, axis=0)
    for leaf in range(part_ref.shape[0] // LEAF):
        rows = slice(leaf * LEAF, (leaf + 1) * LEAF)
        basis = jnp.concatenate([bases_ref[level, rows, :] for level in order], axis=1)
        first = part_ref[rows, :] + jnp.dot(basis, coeffs, preferred_element_type=F32)
        buf[rows, :] = weighted(weights_ref, first, rows)
        out_ref[rows, :] = jnp.dot(leaves_ref[rows, :], buf[rows, :], preferred_element_type=F32)


def near_result_kernel(factors, oriented_ref, high_ref, low_ref, other_ref, bases_ref, part_ref, out_ref):
    pieces = [
        own_coefficients(oriented_ref, 0, high_ref[...], factors),
        own_coefficients(oriented_ref, 1, low_ref[...], factors),
        other_coefficients(oriented_ref, 1, other_ref[...], factors),
    ]
    order = [own_level(0), own_level(1), other_level(1)]
    basis = jnp.concatenate([bases_ref[level] for level in order], axis=1)
    coeffs = jnp.concatenate(pieces, axis=0)
    out_ref[...] = part_ref[...] + jnp.dot(basis, coeffs, preferred_element_type=F32)


def result_kernel(factors, oriented_ref, other_ref, bases_ref, part_ref, result_ref, buf, sems):
    coeffs = other_coefficients(oriented_ref, 0, other_ref[...], factors)
    copies = []
    for chunk in range(part_ref.shape[0] // CHUNK):
        rows = pl.ds(chunk * CHUNK, CHUNK)
        basis = bases_ref[other_level(0), rows, :]
        total = part_ref[rows, :] + jnp.dot(basis, coeffs, preferred_element_type=F32)
        buf[rows, :] = total.astype(BF16)
        copies.append(pltpu.make_async_copy(buf.at[rows, :], result_ref.at[rows, :], sems.at[chunk]))
        copies[-1].start()
    for copy in copies:
        copy.wait()


def on_device(signal, leaves, bases, couplings, weights):
    count = lax.axis_size(AXIS)
    bits = index_bits()
    rows_dev, width = signal.shape
    levels, _, rank = bases.shape
    odd = parity_of() == 1
    far1, far2, far3, far4 = (1 << (bits - level - 1) for level in range(levels))
    factors = [1.0 / math.sqrt(rows_dev * (count >> level + 1) * rank) for level in range(levels)]
    weight_rows = weights.reshape(rows_dev // SPAN, SPAN)
    mults = rows_dev * width * rank * 2
    chunks = rows_dev // CHUNK
    sums_shape = jax.ShapeDtypeStruct((rank, width), F32)
    pair_shape = jax.ShapeDtypeStruct((2, rank, width), F32)
    part_shape = jax.ShapeDtypeStruct((rows_dev, width), F32)
    gram_shape = jax.ShapeDtypeStruct((levels * rank, 2 * rank), F32)

    def swap(value, odd_mask, even_mask):
        pairs = [(source, source ^ (odd_mask if source % 2 else even_mask)) for source in range(count)]
        return lax.ppermute(value, AXIS, pairs)

    def beside(arrays, *riders):
        return lax.optimization_barrier((*arrays, *riders))

    def begin(send, high, low):
        got = swap(send, 1, 1)
        high = high + got[0]
        low = low + got[1]
        for bit in range(1, bits - levels):
            high = high + swap(high, 1 << bit, 1 << bit)
            low = low + swap(low, 1 << bit, 1 << bit)
        return high, low

    def rounds(high, low, rider_one, rider_two, rider_three, passenger=None):
        near = swap(high, far1, far3)
        across = swap(high, far1 | far2, far4)
        near, across, *ridden = beside((near, across), *rider_one())
        high = jnp.where(odd, near + across, high + near)
        got = swap(high, far4, far2)
        low, passenger = beside((swap(low, far3, far4),), ridden.pop() if passenger is None else passenger)
        passenger = swap(passenger, 1, 1)
        got, *ridden = beside((got,), *rider_two(*ridden))
        high = jnp.where(odd, high + got, got)
        low = jnp.where(odd, low + swap(low, far4, far3), low)
        got = swap(high, far3, far4)
        got, *ridden = beside((got,), *rider_three(low, passenger, *ridden))
        return high + got, low, *ridden

    send, bases, signal = call(
        first_kernel,
        [pair_shape, jax.ShapeDtypeStruct(bases.shape, BF16), jax.ShapeDtypeStruct(signal.shape, BF16)],
        [pltpu.with_memory_space_constraint(array, pltpu.HBM) for array in (bases, signal)],
        2 * mults,
        arrays_in=HBM,
        scratch=[pltpu.SemaphoreType.DMA((5,))],
    )
    kept = call(kept_kernel, [sums_shape] * 2, [bases, signal], 2 * mults)

    def first_riders():
        oriented, turned = call(
            prepare_kernel,
            [
                jax.ShapeDtypeStruct((levels, rank, rank), BF16),
                jax.ShapeDtypeStruct((levels * rank, rows_dev), BF16),
            ],
            [couplings, bases],
            mults,
        )
        keep, send = call(gram_kernel, [gram_shape] * 2, [bases, weight_rows, turned], 2 * levels * mults)
        return oriented, turned, keep, send

    def second_riders(oriented, turned, keep):
        (part,) = call(near_kernel, [part_shape], [leaves, signal], LEAF // rank * mults)
        return oriented, turned, keep, part

    def third_riders(low, got, oriented, turned, keep, part):
        sums, gram = call(
            functools.partial(low_kernel, factors),
            [
                jax.ShapeDtypeStruct((levels * rank, width), F32),
                jax.ShapeDtypeStruct((levels * rank, 2 * rank), BF16),
            ],
            [oriented, low, keep, got, part, weight_rows, turned],
            (1 + levels) * mults,
        )
        return oriented, part, sums, gram

    high, low, oriented, part, sums, gram = rounds(
        *begin(send, *kept), first_riders, second_riders, third_riders
    )
    high, low_other = beside((high, swap(low, 1, 1)))
    send, *kept = call(
        functools.partial(middle_kernel, factors),
        [pair_shape, sums_shape, sums_shape],
        [oriented, high, gram, sums],
        mults,
    )
    next_high, next_low, high, low = beside(begin(send, *kept), high, low)

    def second_part(_, high_other):
        return call(
            functools.partial(second_part_kernel, factors),
            [part_shape],
            [oriented, high, low, high_other, low_other, bases, part, weight_rows, leaves],
            (LEAF // rank + levels) * mults,
            scratch=[pltpu.VMEM((rows_dev, width), BF16)],
        )

    high, low, part = rounds(next_high, next_low, tuple, tuple, second_part, high)
    low_other, high_other = swap(low, 1, 1), swap(high, 1, 1)
    (part,) = call(
        functools.partial(near_result_kernel, factors),
        [part_shape],
        [oriented, high, low, low_other, bases, part],
        3 * mults,
    )
    (result,) = call(
        functools.partial(result_kernel, factors),
        [jax.ShapeDtypeStruct((rows_dev, width), BF16)],
        [oriented, high_other, bases, part],
        mults,
        outs_in=HBM,
        scratch=[pltpu.VMEM((rows_dev, width), BF16), pltpu.SemaphoreType.DMA((chunks,))],
    )
    return result


def solution(mesh):
    in_specs = (P("rows", None), P("rows", None), P(None, "rows", None), P(), P("rows"))
    out_specs = P("rows", None)
    return jax.shard_map(
        on_device, mesh=mesh, in_specs=in_specs, out_specs=out_specs, check_vma=False
    )
```

```python
import functools
import math

import jax
import jax.numpy as jnp
from jax import lax
from jax.experimental import pallas as pl
from jax.experimental.pallas import tpu as pltpu
from jax.sharding import PartitionSpec as P

AXIS = "rows"
LEAF = 512
CHUNK = 256
SPAN = 128
F32 = jnp.float32
BF16 = jnp.bfloat16


VMEM = pl.BlockSpec(memory_space=pltpu.VMEM)
HBM = pl.BlockSpec(memory_space=pltpu.HBM)


def call(kernel, outs, arrays, flops, arrays_in=VMEM, outs_in=VMEM, scratch=()):
    moved = sum(math.prod(a.shape) * a.dtype.itemsize for a in (*arrays, *outs))
    return pl.pallas_call(
        kernel,
        out_shape=outs,
        in_specs=[arrays_in] * len(arrays),
        out_specs=[outs_in] * len(outs),
        scratch_shapes=scratch,
        compiler_params=pltpu.CompilerParams(vmem_limit_bytes=24 * 2**20),
        cost_estimate=pl.CostEstimate(flops=flops, bytes_accessed=moved, transcendentals=0),
    )(*arrays)


def index_bits():
    return lax.axis_size(AXIS).bit_length() - 1


def transposed_dot(basis, vec):
    return lax.dot_general(basis, vec, (((0,), (0,)), ((), ())), preferred_element_type=F32)


def parity_of():
    return lax.axis_index(AXIS) % 2


def own_level(slot):
    return 1 - parity_of() + 2 * slot


def other_level(slot):
    return parity_of() + 2 * slot


def first_kernel(bases_in, vec_in, send_high_ref, vec_ref, basis_buf, sems):
    copies = [
        pltpu.make_async_copy(vec_in, vec_ref, sems.at[0]),
        pltpu.make_async_copy(bases_in.at[other_level(0)], basis_buf, sems.at[1]),
    ]
    for copy in copies:
        copy.start()
    for copy in copies:
        copy.wait()
    send_high_ref[...] = transposed_dot(basis_buf[...], vec_ref[...])


def kept_kernel(bases_ref, vec_ref, send_low_ref, high_ref, low_ref):
    rank = bases_ref.shape[2]
    order = [other_level(1), own_level(0), own_level(1)]
    basis = jnp.concatenate([bases_ref[level] for level in order], axis=1)
    proj = transposed_dot(basis, vec_ref[...])
    send_low_ref[...] = proj[:rank]
    high_ref[...] = proj[rank : 2 * rank]
    low_ref[...] = proj[2 * rank :]


def prepare_kernel(couplings_ref, bases_ref, oriented_ref, turned_ref):
    myself = lax.axis_index(AXIS)
    bits = index_bits()
    rank = bases_ref.shape[2]
    for level in range(bases_ref.shape[0]):
        coupling = couplings_ref[(1 << level) - 1 + (myself >> bits - level)].astype(F32)
        side = myself >> bits - level - 1 & 1
        oriented_ref[level] = jnp.where(side == 0, coupling, coupling.T).astype(BF16)
    for slot in range(2):
        turned_ref[pl.ds(slot * rank, rank), :] = bases_ref[other_level(slot)].T
        turned_ref[pl.ds((2 + slot) * rank, rank), :] = bases_ref[own_level(slot)].T


def weighted(weights_ref, values, rows):
    columns = weights_ref[...].T
    blocks = range(rows.start // SPAN, rows.stop // SPAN)
    column = jnp.concatenate([columns[:, block : block + 1] for block in blocks], axis=0)
    return (column * values).astype(BF16)


def near_kernel(leaves_ref, vec_ref, part_ref):
    for leaf in range(vec_ref.shape[0] // LEAF):
        rows = slice(leaf * LEAF, (leaf + 1) * LEAF)
        part_ref[rows, :] = jnp.dot(leaves_ref[rows, :], vec_ref[rows, :], preferred_element_type=F32)


def gram_kernel(bases_ref, weights_ref, turned_ref, keep_ref, send_ref):
    rank, rows_dev = bases_ref.shape[2], bases_ref.shape[1]
    total = None
    for chunk in range(rows_dev // CHUNK):
        rows = slice(chunk * CHUNK, (chunk + 1) * CHUNK)
        order = [other_level(slot) for slot in range(2)] + [own_level(slot) for slot in range(2)]
        basis = jnp.concatenate([bases_ref[level, rows, :] for level in order], axis=1)
        basis = weighted(weights_ref, basis.astype(F32), rows)
        term = jnp.dot(turned_ref[:, rows], basis, preferred_element_type=F32)
        total = term if total is None else total + term
    keep_ref[...] = total[:, 2 * rank :]
    send_ref[: 2 * rank, :] = total[2 * rank :, : 2 * rank]
    send_ref[2 * rank :, :] = total[: 2 * rank, : 2 * rank]


def coefficients(oriented_ref, level, factor, sums):
    quotient = (sums * factor).astype(BF16)
    return jnp.dot(oriented_ref[level], quotient, preferred_element_type=F32).astype(BF16)


def own_coefficients(oriented_ref, slot, sums, factors):
    factor = jnp.where(parity_of() == 1, factors[2 * slot], factors[2 * slot + 1])
    return coefficients(oriented_ref, own_level(slot), factor, sums)


def other_coefficients(oriented_ref, slot, sums, factors):
    factor = jnp.where(parity_of() == 1, factors[2 * slot + 1], factors[2 * slot])
    return coefficients(oriented_ref, other_level(slot), factor, sums)


def low_kernel(
    factors, oriented_ref, low_ref, keep_ref, got_ref, part_ref, weights_ref, turned_ref, sums_ref, gram_ref
):
    gram = keep_ref[...] + got_ref[...]
    rough = gram.astype(BF16)
    rest = (gram - rough.astype(F32)).astype(BF16)
    rank = low_ref.shape[0]
    both = jnp.concatenate([rough[:, rank:], rest[:, rank:]], axis=1)
    coeffs = own_coefficients(oriented_ref, 1, low_ref[...], factors)
    total = jnp.dot(both, jnp.concatenate([coeffs] * 2, axis=0), preferred_element_type=F32)
    for leaf in range(part_ref.shape[0] // LEAF):
        rows = slice(leaf * LEAF, (leaf + 1) * LEAF)
        near = weighted(weights_ref, part_ref[rows, :], rows)
        total = total + jnp.dot(turned_ref[:, rows], near, preferred_element_type=F32)
    sums_ref[...] = total
    gram_ref[:, :rank] = rough[:, :rank]
    gram_ref[:, rank:] = rest[:, :rank]


def middle_kernel(factors, oriented_ref, high_ref, gram_ref, sums_ref, send_high_ref, send_low_ref, keep_high_ref, keep_low_ref):
    coeffs = own_coefficients(oriented_ref, 0, high_ref[...], factors)
    delta = jnp.dot(gram_ref[...], jnp.concatenate([coeffs] * 2, axis=0), preferred_element_type=F32)
    proj = sums_ref[...] + delta
    rank = high_ref.shape[0]
    send_high_ref[...] = proj[:rank]
    send_low_ref[...] = proj[rank : 2 * rank]
    keep_high_ref[...] = proj[2 * rank : 3 * rank]
    keep_low_ref[...] = proj[3 * rank :]


def second_part_kernel(
    factors, oriented_ref, high_ref, low_ref, high_other_ref, low_other_ref, bases_ref, part_ref, weights_ref, leaves_ref, out_ref, buf
):
    pieces = []
    order = []
    for slot, (own_ref, other_ref) in enumerate(((high_ref, high_other_ref), (low_ref, low_other_ref))):
        pieces += [own_coefficients(oriented_ref, slot, own_ref[...], factors)]
        pieces += [other_coefficients(oriented_ref, slot, other_ref[...], factors)]
        order += [own_level(slot), other_level(slot)]
    coeffs = jnp.concatenate(pieces, axis=0)
    for leaf in range(part_ref.shape[0] // LEAF):
        rows = slice(leaf * LEAF, (leaf + 1) * LEAF)
        basis = jnp.concatenate([bases_ref[level, rows, :] for level in order], axis=1)
        first = part_ref[rows, :] + jnp.dot(basis, coeffs, preferred_element_type=F32)
        buf[rows, :] = weighted(weights_ref, first, rows)
        out_ref[rows, :] = jnp.dot(leaves_ref[rows, :], buf[rows, :], preferred_element_type=F32)


def near_result_kernel(factors, oriented_ref, high_ref, low_ref, other_ref, bases_ref, part_ref, out_ref):
    pieces = [
        own_coefficients(oriented_ref, 0, high_ref[...], factors),
        own_coefficients(oriented_ref, 1, low_ref[...], factors),
        other_coefficients(oriented_ref, 1, other_ref[...], factors),
    ]
    order = [own_level(0), own_level(1), other_level(1)]
    basis = jnp.concatenate([bases_ref[level] for level in order], axis=1)
    coeffs = jnp.concatenate(pieces, axis=0)
    out_ref[...] = part_ref[...] + jnp.dot(basis, coeffs, preferred_element_type=F32)


def result_kernel(factors, oriented_ref, other_ref, bases_ref, part_ref, result_ref, buf, sems):
    coeffs = other_coefficients(oriented_ref, 0, other_ref[...], factors)
    copies = []
    for chunk in range(part_ref.shape[0] // CHUNK):
        rows = pl.ds(chunk * CHUNK, CHUNK)
        basis = bases_ref[other_level(0), rows, :]
        total = part_ref[rows, :] + jnp.dot(basis, coeffs, preferred_element_type=F32)
        buf[rows, :] = total.astype(BF16)
        copies.append(pltpu.make_async_copy(buf.at[rows, :], result_ref.at[rows, :], sems.at[chunk]))
        copies[-1].start()
    for copy in copies:
        copy.wait()


def on_device(signal, leaves, bases, couplings, weights):
    count = lax.axis_size(AXIS)
    bits = index_bits()
    rows_dev, width = signal.shape
    levels, _, rank = bases.shape
    odd = parity_of() == 1
    far1, far2, far3, far4 = (1 << (bits - level - 1) for level in range(levels))
    factors = [1.0 / math.sqrt(rows_dev * (count >> level + 1) * rank) for level in range(levels)]
    weight_rows = weights.reshape(rows_dev // SPAN, SPAN)
    mults = rows_dev * width * rank * 2
    chunks = rows_dev // CHUNK
    sums_shape = jax.ShapeDtypeStruct((rank, width), F32)
    pair_shape = jax.ShapeDtypeStruct((2, rank, width), F32)
    part_shape = jax.ShapeDtypeStruct((rows_dev, width), F32)
    gram_shape = jax.ShapeDtypeStruct((levels * rank, 2 * rank), F32)

    def swap(value, odd_mask, even_mask):
        pairs = [(source, source ^ (odd_mask if source % 2 else even_mask)) for source in range(count)]
        return lax.ppermute(value, AXIS, pairs)

    def beside(arrays, *riders):
        return lax.optimization_barrier((*arrays, *riders))

    def begin(send_high, send_low, high, low):
        high = high + swap(send_high, 1, 1)
        low = low + swap(send_low, 1, 1)
        for bit in range(1, bits - levels):
            high = high + swap(high, 1 << bit, 1 << bit)
            low = low + swap(low, 1 << bit, 1 << bit)
        return high, low

    def rounds(high, low, rider_one, rider_two, rider_three, passenger=None):
        near = swap(high, far1, far3)
        across = swap(high, far1 | far2, far4)
        near, across, *ridden = beside((near, across), *rider_one())
        high = jnp.where(odd, near + across, high + near)
        got = swap(high, far4, far2)
        low, passenger = beside((swap(low, far3, far4),), ridden.pop() if passenger is None else passenger)
        passenger = swap(passenger, 1, 1)
        got, *ridden = beside((got,), *rider_two(*ridden))
        high = jnp.where(odd, high + got, got)
        low = jnp.where(odd, low + swap(low, far4, far3), low)
        got = swap(high, far3, far4)
        got, *ridden = beside((got,), *rider_three(low, passenger, *ridden))
        return high + got, low, *ridden

    send_high, signal = call(
        first_kernel,
        [sums_shape, jax.ShapeDtypeStruct(signal.shape, BF16)],
        [pltpu.with_memory_space_constraint(array, pltpu.HBM) for array in (bases, signal)],
        mults,
        arrays_in=HBM,
        scratch=[pltpu.VMEM((rows_dev, rank), BF16), pltpu.SemaphoreType.DMA((2,))],
    )
    kept = call(kept_kernel, [sums_shape] * 3, [bases, signal], 3 * mults)

    def first_riders():
        oriented, turned = call(
            prepare_kernel,
            [
                jax.ShapeDtypeStruct((levels, rank, rank), BF16),
                jax.ShapeDtypeStruct((levels * rank, rows_dev), BF16),
            ],
            [couplings, bases],
            mults,
        )
        keep, send = call(gram_kernel, [gram_shape] * 2, [bases, weight_rows, turned], 2 * levels * mults)
        return oriented, turned, keep, send

    def second_riders(oriented, turned, keep):
        (part,) = call(near_kernel, [part_shape], [leaves, signal], LEAF // rank * mults)
        return oriented, turned, keep, part

    def third_riders(low, got, oriented, turned, keep, part):
        sums, gram = call(
            functools.partial(low_kernel, factors),
            [
                jax.ShapeDtypeStruct((levels * rank, width), F32),
                jax.ShapeDtypeStruct((levels * rank, 2 * rank), BF16),
            ],
            [oriented, low, keep, got, part, weight_rows, turned],
            (1 + levels) * mults,
        )
        return oriented, part, sums, gram

    high, low, oriented, part, sums, gram = rounds(
        *begin(send_high, *kept), first_riders, second_riders, third_riders
    )
    high, low_other = beside((high, swap(low, 1, 1)))
    kept = call(
        functools.partial(middle_kernel, factors),
        [sums_shape] * 4,
        [oriented, high, gram, sums],
        mults,
    )
    next_high, next_low, high, low = beside(begin(*kept), high, low)

    def second_part(_, high_other):
        return call(
            functools.partial(second_part_kernel, factors),
            [part_shape],
            [oriented, high, low, high_other, low_other, bases, part, weight_rows, leaves],
            (LEAF // rank + levels) * mults,
            scratch=[pltpu.VMEM((rows_dev, width), BF16)],
        )

    high, low, part = rounds(next_high, next_low, tuple, tuple, second_part, high)
    low_other, high_other = swap(low, 1, 1), swap(high, 1, 1)
    (part,) = call(
        functools.partial(near_result_kernel, factors),
        [part_shape],
        [oriented, high, low, low_other, bases, part],
        3 * mults,
    )
    (result,) = call(
        functools.partial(result_kernel, factors),
        [jax.ShapeDtypeStruct((rows_dev, width), BF16)],
        [oriented, high_other, bases, part],
        mults,
        outs_in=HBM,
        scratch=[pltpu.VMEM((rows_dev, width), BF16), pltpu.SemaphoreType.DMA((chunks,))],
    )
    return result


def solution(mesh):
    in_specs = (P("rows", None), P("rows", None), P(None, "rows", None), P(), P("rows"))
    out_specs = P("rows", None)
    return jax.shard_map(
        on_device, mesh=mesh, in_specs=in_specs, out_specs=out_specs, check_vma=False
    )
```

```python
import functools
import math

import jax
import jax.numpy as jnp
from jax import lax
from jax.experimental import pallas as pl
from jax.experimental.pallas import tpu as pltpu
from jax.sharding import PartitionSpec as P

AXIS = "rows"
LEAF = 512
CHUNK = 256
SPAN = 128
F32 = jnp.float32
BF16 = jnp.bfloat16


VMEM = pl.BlockSpec(memory_space=pltpu.VMEM)
HBM = pl.BlockSpec(memory_space=pltpu.HBM)


def call(kernel, outs, arrays, flops, arrays_in=VMEM, outs_in=VMEM, scratch=()):
    moved = sum(math.prod(a.shape) * a.dtype.itemsize for a in (*arrays, *outs))
    return pl.pallas_call(
        kernel,
        out_shape=outs,
        in_specs=[arrays_in] * len(arrays),
        out_specs=[outs_in] * len(outs),
        scratch_shapes=scratch,
        compiler_params=pltpu.CompilerParams(vmem_limit_bytes=24 * 2**20),
        cost_estimate=pl.CostEstimate(flops=flops, bytes_accessed=moved, transcendentals=0),
    )(*arrays)


def index_bits():
    return lax.axis_size(AXIS).bit_length() - 1


def transposed_dot(basis, vec):
    return lax.dot_general(basis, vec, (((0,), (0,)), ((), ())), preferred_element_type=F32)


def parity_of():
    return lax.axis_index(AXIS) % 2


def own_level(slot):
    return 1 - parity_of() + 2 * slot


def other_level(slot):
    return parity_of() + 2 * slot


def first_kernel(bases_in, vec_in, send_high_ref, vec_ref, basis_buf, sems):
    copies = [
        pltpu.make_async_copy(vec_in, vec_ref, sems.at[0]),
        pltpu.make_async_copy(bases_in.at[other_level(0)], basis_buf, sems.at[1]),
    ]
    for copy in copies:
        copy.start()
    for copy in copies:
        copy.wait()
    send_high_ref[...] = transposed_dot(basis_buf[...], vec_ref[...])


def kept_kernel(bases_ref, vec_ref, send_low_ref, high_ref, low_ref):
    rank = bases_ref.shape[2]
    order = [other_level(1), own_level(0), own_level(1)]
    basis = jnp.concatenate([bases_ref[level] for level in order], axis=1)
    proj = transposed_dot(basis, vec_ref[...])
    send_low_ref[...] = proj[:rank]
    high_ref[...] = proj[rank : 2 * rank]
    low_ref[...] = proj[2 * rank :]


def prepare_kernel(couplings_ref, bases_ref, oriented_ref, turned_ref):
    myself = lax.axis_index(AXIS)
    bits = index_bits()
    rank = bases_ref.shape[2]
    for level in range(bases_ref.shape[0]):
        coupling = couplings_ref[(1 << level) - 1 + (myself >> bits - level)].astype(F32)
        side = myself >> bits - level - 1 & 1
        oriented_ref[level] = jnp.where(side == 0, coupling, coupling.T).astype(BF16)
    for slot in range(2):
        turned_ref[pl.ds(slot * rank, rank), :] = bases_ref[other_level(slot)].T
        turned_ref[pl.ds((2 + slot) * rank, rank), :] = bases_ref[own_level(slot)].T


def weighted(weights_ref, values, rows):
    columns = weights_ref[...].T
    blocks = range(rows.start // SPAN, rows.stop // SPAN)
    column = jnp.concatenate([columns[:, block : block + 1] for block in blocks], axis=0)
    return (column * values).astype(BF16)


def near_kernel(leaves_ref, vec_ref, part_ref):
    for leaf in range(vec_ref.shape[0] // LEAF):
        rows = slice(leaf * LEAF, (leaf + 1) * LEAF)
        part_ref[rows, :] = jnp.dot(leaves_ref[rows, :], vec_ref[rows, :], preferred_element_type=F32)


def gram_kernel(bases_ref, weights_ref, turned_ref, keep_ref, send_ref):
    rank, rows_dev = bases_ref.shape[2], bases_ref.shape[1]
    total = None
    for chunk in range(rows_dev // CHUNK):
        rows = slice(chunk * CHUNK, (chunk + 1) * CHUNK)
        order = [other_level(slot) for slot in range(2)] + [own_level(slot) for slot in range(2)]
        basis = jnp.concatenate([bases_ref[level, rows, :] for level in order], axis=1)
        basis = weighted(weights_ref, basis.astype(F32), rows)
        term = jnp.dot(turned_ref[:, rows], basis, preferred_element_type=F32)
        total = term if total is None else total + term
    keep_ref[...] = total[:, 2 * rank :]
    send_ref[: 2 * rank, :] = total[2 * rank :, : 2 * rank]
    send_ref[2 * rank :, :] = total[: 2 * rank, : 2 * rank]


def coefficients(oriented_ref, level, factor, sums):
    quotient = (sums * factor).astype(BF16)
    return jnp.dot(oriented_ref[level], quotient, preferred_element_type=F32).astype(BF16)


def own_coefficients(oriented_ref, slot, sums, factors):
    factor = jnp.where(parity_of() == 1, factors[2 * slot], factors[2 * slot + 1])
    return coefficients(oriented_ref, own_level(slot), factor, sums)


def other_coefficients(oriented_ref, slot, sums, factors):
    factor = jnp.where(parity_of() == 1, factors[2 * slot + 1], factors[2 * slot])
    return coefficients(oriented_ref, other_level(slot), factor, sums)


def low_kernel(
    factors, oriented_ref, low_ref, keep_ref, got_ref, part_ref, weights_ref, turned_ref, sums_ref, gram_ref
):
    gram = keep_ref[...] + got_ref[...]
    rough = gram.astype(BF16)
    rest = (gram - rough.astype(F32)).astype(BF16)
    rank = low_ref.shape[0]
    both = jnp.concatenate([rough[:, rank:], rest[:, rank:]], axis=1)
    coeffs = own_coefficients(oriented_ref, 1, low_ref[...], factors)
    total = jnp.dot(both, jnp.concatenate([coeffs] * 2, axis=0), preferred_element_type=F32)
    for leaf in range(part_ref.shape[0] // LEAF):
        rows = slice(leaf * LEAF, (leaf + 1) * LEAF)
        near = weighted(weights_ref, part_ref[rows, :], rows)
        total = total + jnp.dot(turned_ref[:, rows], near, preferred_element_type=F32)
    sums_ref[...] = total
    gram_ref[:, :rank] = rough[:, :rank]
    gram_ref[:, rank:] = rest[:, :rank]


def middle_kernel(factors, oriented_ref, high_ref, gram_ref, sums_ref, send_high_ref, send_low_ref, keep_high_ref, keep_low_ref):
    coeffs = own_coefficients(oriented_ref, 0, high_ref[...], factors)
    delta = jnp.dot(gram_ref[...], jnp.concatenate([coeffs] * 2, axis=0), preferred_element_type=F32)
    proj = sums_ref[...] + delta
    rank = high_ref.shape[0]
    send_high_ref[...] = proj[:rank]
    send_low_ref[...] = proj[rank : 2 * rank]
    keep_high_ref[...] = proj[2 * rank : 3 * rank]
    keep_low_ref[...] = proj[3 * rank :]


def second_part_kernel(
    factors, oriented_ref, high_ref, low_ref, high_other_ref, low_other_ref, bases_ref, part_ref, weights_ref, leaves_ref, out_ref, buf
):
    pieces = []
    order = []
    for slot, (own_ref, other_ref) in enumerate(((high_ref, high_other_ref), (low_ref, low_other_ref))):
        pieces += [own_coefficients(oriented_ref, slot, own_ref[...], factors)]
        pieces += [other_coefficients(oriented_ref, slot, other_ref[...], factors)]
        order += [own_level(slot), other_level(slot)]
    coeffs = jnp.concatenate(pieces, axis=0)
    for leaf in range(part_ref.shape[0] // LEAF):
        rows = slice(leaf * LEAF, (leaf + 1) * LEAF)
        basis = jnp.concatenate([bases_ref[level, rows, :] for level in order], axis=1)
        first = part_ref[rows, :] + jnp.dot(basis, coeffs, preferred_element_type=F32)
        buf[rows, :] = weighted(weights_ref, first, rows)
        out_ref[rows, :] = jnp.dot(leaves_ref[rows, :], buf[rows, :], preferred_element_type=F32)


def near_result_kernel(factors, oriented_ref, high_ref, low_ref, other_ref, bases_ref, part_ref, out_ref):
    pieces = [
        own_coefficients(oriented_ref, 0, high_ref[...], factors),
        own_coefficients(oriented_ref, 1, low_ref[...], factors),
        other_coefficients(oriented_ref, 1, other_ref[...], factors),
    ]
    order = [own_level(0), own_level(1), other_level(1)]
    basis = jnp.concatenate([bases_ref[level] for level in order], axis=1)
    coeffs = jnp.concatenate(pieces, axis=0)
    out_ref[...] = part_ref[...] + jnp.dot(basis, coeffs, preferred_element_type=F32)


def result_kernel(factors, oriented_ref, other_ref, bases_ref, part_ref, result_ref, buf, sems):
    coeffs = other_coefficients(oriented_ref, 0, other_ref[...], factors)
    copies = []
    for chunk in range(part_ref.shape[0] // CHUNK):
        rows = pl.ds(chunk * CHUNK, CHUNK)
        basis = bases_ref[other_level(0), rows, :]
        total = part_ref[rows, :] + jnp.dot(basis, coeffs, preferred_element_type=F32)
        buf[rows, :] = total.astype(BF16)
        copies.append(pltpu.make_async_copy(buf.at[rows, :], result_ref.at[rows, :], sems.at[chunk]))
        copies[-1].start()
    for copy in copies:
        copy.wait()


def on_device(signal, leaves, bases, couplings, weights):
    count = lax.axis_size(AXIS)
    bits = index_bits()
    rows_dev, width = signal.shape
    levels, _, rank = bases.shape
    odd = parity_of() == 1
    far1, far2, far3, far4 = (1 << (bits - level - 1) for level in range(levels))
    factors = [1.0 / math.sqrt(rows_dev * (count >> level + 1) * rank) for level in range(levels)]
    weight_rows = weights.reshape(rows_dev // SPAN, SPAN)
    mults = rows_dev * width * rank * 2
    chunks = rows_dev // CHUNK
    sums_shape = jax.ShapeDtypeStruct((rank, width), F32)
    pair_shape = jax.ShapeDtypeStruct((2, rank, width), F32)
    part_shape = jax.ShapeDtypeStruct((rows_dev, width), F32)
    gram_shape = jax.ShapeDtypeStruct((levels * rank, 2 * rank), F32)

    def swap(value, odd_mask, even_mask):
        pairs = [(source, source ^ (odd_mask if source % 2 else even_mask)) for source in range(count)]
        return lax.ppermute(value, AXIS, pairs)

    def beside(arrays, *riders):
        return lax.optimization_barrier((*arrays, *riders))

    def begin(send_high, send_low, high, low):
        high = high + swap(send_high, 1, 1)
        low = low + swap(send_low, 1, 1)
        for bit in range(1, bits - levels):
            high = high + swap(high, 1 << bit, 1 << bit)
            low = low + swap(low, 1 << bit, 1 << bit)
        return high, low

    def rounds(high, low, rider_one, rider_two, rider_three, passenger=None):
        near = swap(high, far1, far3)
        across = swap(high, far1 | far2, far4)
        near, across, *ridden = beside((near, across), *rider_one())
        high = jnp.where(odd, near + across, high + near)
        got = swap(high, far4, far2)
        passenger = ridden.pop() if passenger is None else passenger
        low, passenger, *ridden = beside((swap(low, far3, far4),), passenger, *rider_two(*ridden))
        passenger = swap(passenger, 1, 1)
        high = jnp.where(odd, high + got, got)
        low = jnp.where(odd, low + swap(low, far4, far3), low)
        got = swap(high, far3, far4)
        got, *ridden = beside((got,), *rider_three(low, passenger, *ridden))
        return high + got, low, *ridden

    send_high, signal = call(
        first_kernel,
        [sums_shape, jax.ShapeDtypeStruct(signal.shape, BF16)],
        [pltpu.with_memory_space_constraint(array, pltpu.HBM) for array in (bases, signal)],
        mults,
        arrays_in=HBM,
        scratch=[pltpu.VMEM((rows_dev, rank), BF16), pltpu.SemaphoreType.DMA((2,))],
    )
    kept = call(kept_kernel, [sums_shape] * 3, [bases, signal], 3 * mults)

    def first_riders():
        oriented, turned = call(
            prepare_kernel,
            [
                jax.ShapeDtypeStruct((levels, rank, rank), BF16),
                jax.ShapeDtypeStruct((levels * rank, rows_dev), BF16),
            ],
            [couplings, bases],
            mults,
        )
        keep, send = call(gram_kernel, [gram_shape] * 2, [bases, weight_rows, turned], 2 * levels * mults)
        return oriented, turned, keep, send

    def second_riders(oriented, turned, keep):
        (part,) = call(near_kernel, [part_shape], [leaves, signal], LEAF // rank * mults)
        return oriented, turned, keep, part

    def third_riders(low, got, oriented, turned, keep, part):
        sums, gram = call(
            functools.partial(low_kernel, factors),
            [
                jax.ShapeDtypeStruct((levels * rank, width), F32),
                jax.ShapeDtypeStruct((levels * rank, 2 * rank), BF16),
            ],
            [oriented, low, keep, got, part, weight_rows, turned],
            (1 + levels) * mults,
        )
        return oriented, part, sums, gram

    high, low, oriented, part, sums, gram = rounds(
        *begin(send_high, *kept), first_riders, second_riders, third_riders
    )
    high, low_other = beside((high, swap(low, 1, 1)))
    kept = call(
        functools.partial(middle_kernel, factors),
        [sums_shape] * 4,
        [oriented, high, gram, sums],
        mults,
    )
    next_high, next_low, high, low = beside(begin(*kept), high, low)

    def second_part(_, high_other):
        return call(
            functools.partial(second_part_kernel, factors),
            [part_shape],
            [oriented, high, low, high_other, low_other, bases, part, weight_rows, leaves],
            (LEAF // rank + levels) * mults,
            scratch=[pltpu.VMEM((rows_dev, width), BF16)],
        )

    high, low, part = rounds(next_high, next_low, tuple, tuple, second_part, high)
    low_other, high_other = swap(low, 1, 1), swap(high, 1, 1)
    (part,) = call(
        functools.partial(near_result_kernel, factors),
        [part_shape],
        [oriented, high, low, low_other, bases, part],
        3 * mults,
    )
    (result,) = call(
        functools.partial(result_kernel, factors),
        [jax.ShapeDtypeStruct((rows_dev, width), BF16)],
        [oriented, high_other, bases, part],
        mults,
        outs_in=HBM,
        scratch=[pltpu.VMEM((rows_dev, width), BF16), pltpu.SemaphoreType.DMA((chunks,))],
    )
    return result


def solution(mesh):
    in_specs = (P("rows", None), P("rows", None), P(None, "rows", None), P(), P("rows"))
    out_specs = P("rows", None)
    return jax.shard_map(
        on_device, mesh=mesh, in_specs=in_specs, out_specs=out_specs, check_vma=False
    )
```

```python
import functools
import math

import jax
import jax.numpy as jnp
from jax import lax
from jax.experimental import pallas as pl
from jax.experimental.pallas import tpu as pltpu
from jax.sharding import PartitionSpec as P

AXIS = "rows"
LEAF = 512
CHUNK = 256
SPAN = 128
F32 = jnp.float32
BF16 = jnp.bfloat16


VMEM = pl.BlockSpec(memory_space=pltpu.VMEM)
HBM = pl.BlockSpec(memory_space=pltpu.HBM)


def call(kernel, outs, arrays, flops, arrays_in=VMEM, outs_in=VMEM, scratch=()):
    moved = sum(math.prod(a.shape) * a.dtype.itemsize for a in (*arrays, *outs))
    return pl.pallas_call(
        kernel,
        out_shape=outs,
        in_specs=[arrays_in] * len(arrays),
        out_specs=[outs_in] * len(outs),
        scratch_shapes=scratch,
        compiler_params=pltpu.CompilerParams(vmem_limit_bytes=24 * 2**20),
        cost_estimate=pl.CostEstimate(flops=flops, bytes_accessed=moved, transcendentals=0),
    )(*arrays)


def index_bits():
    return lax.axis_size(AXIS).bit_length() - 1


def transposed_dot(basis, vec):
    return lax.dot_general(basis, vec, (((0,), (0,)), ((), ())), preferred_element_type=F32)


def parity_of():
    return lax.axis_index(AXIS) % 2


def own_level(slot):
    return 1 - parity_of() + 2 * slot


def other_level(slot):
    return parity_of() + 2 * slot


def first_kernel(bases_in, vec_in, send_high_ref, vec_ref, basis_buf, sems):
    copies = [
        pltpu.make_async_copy(vec_in, vec_ref, sems.at[0]),
        pltpu.make_async_copy(bases_in.at[other_level(0)], basis_buf, sems.at[1]),
    ]
    for copy in copies:
        copy.start()
    for copy in copies:
        copy.wait()
    send_high_ref[...] = transposed_dot(basis_buf[...], vec_ref[...])


def kept_kernel(bases_ref, vec_ref, send_low_ref, high_ref, low_ref):
    rank = bases_ref.shape[2]
    order = [other_level(1), own_level(0), own_level(1)]
    basis = jnp.concatenate([bases_ref[level] for level in order], axis=1)
    proj = transposed_dot(basis, vec_ref[...])
    send_low_ref[...] = proj[:rank]
    high_ref[...] = proj[rank : 2 * rank]
    low_ref[...] = proj[2 * rank :]


def prepare_kernel(couplings_ref, bases_ref, oriented_ref, turned_ref):
    myself = lax.axis_index(AXIS)
    bits = index_bits()
    rank = bases_ref.shape[2]
    for level in range(bases_ref.shape[0]):
        coupling = couplings_ref[(1 << level) - 1 + (myself >> bits - level)].astype(F32)
        side = myself >> bits - level - 1 & 1
        oriented_ref[level] = jnp.where(side == 0, coupling, coupling.T).astype(BF16)
    for slot in range(2):
        turned_ref[pl.ds(slot * rank, rank), :] = bases_ref[other_level(slot)].T
        turned_ref[pl.ds((2 + slot) * rank, rank), :] = bases_ref[own_level(slot)].T


def weighted(weights_ref, values, rows):
    columns = weights_ref[...].T
    blocks = range(rows.start // SPAN, rows.stop // SPAN)
    column = jnp.concatenate([columns[:, block : block + 1] for block in blocks], axis=0)
    return (column * values).astype(BF16)


def near_kernel(leaves_ref, vec_ref, part_ref):
    for leaf in range(vec_ref.shape[0] // LEAF):
        rows = slice(leaf * LEAF, (leaf + 1) * LEAF)
        part_ref[rows, :] = jnp.dot(leaves_ref[rows, :], vec_ref[rows, :], preferred_element_type=F32)


def gram_kernel(bases_ref, weights_ref, turned_ref, keep_ref, send_ref):
    rank, rows_dev = bases_ref.shape[2], bases_ref.shape[1]
    total = None
    for chunk in range(rows_dev // CHUNK):
        rows = slice(chunk * CHUNK, (chunk + 1) * CHUNK)
        order = [other_level(slot) for slot in range(2)] + [own_level(slot) for slot in range(2)]
        basis = jnp.concatenate([bases_ref[level, rows, :] for level in order], axis=1)
        basis = weighted(weights_ref, basis.astype(F32), rows)
        term = jnp.dot(turned_ref[:, rows], basis, preferred_element_type=F32)
        total = term if total is None else total + term
    keep_ref[...] = total[:, 2 * rank :]
    send_ref[: 2 * rank, :] = total[2 * rank :, : 2 * rank]
    send_ref[2 * rank :, :] = total[: 2 * rank, : 2 * rank]


def coefficients(oriented_ref, level, factor, sums):
    quotient = (sums * factor).astype(BF16)
    return jnp.dot(oriented_ref[level], quotient, preferred_element_type=F32).astype(BF16)


def own_coefficients(oriented_ref, slot, sums, factors):
    factor = jnp.where(parity_of() == 1, factors[2 * slot], factors[2 * slot + 1])
    return coefficients(oriented_ref, own_level(slot), factor, sums)


def other_coefficients(oriented_ref, slot, sums, factors):
    factor = jnp.where(parity_of() == 1, factors[2 * slot + 1], factors[2 * slot])
    return coefficients(oriented_ref, other_level(slot), factor, sums)


def low_kernel(
    factors, oriented_ref, low_ref, keep_ref, got_ref, part_ref, weights_ref, turned_ref, sums_ref, gram_ref
):
    gram = keep_ref[...] + got_ref[...]
    rough = gram.astype(BF16)
    rest = (gram - rough.astype(F32)).astype(BF16)
    rank = low_ref.shape[0]
    both = jnp.concatenate([rough[:, rank:], rest[:, rank:]], axis=1)
    coeffs = own_coefficients(oriented_ref, 1, low_ref[...], factors)
    total = jnp.dot(both, jnp.concatenate([coeffs] * 2, axis=0), preferred_element_type=F32)
    for leaf in range(part_ref.shape[0] // LEAF):
        rows = slice(leaf * LEAF, (leaf + 1) * LEAF)
        near = weighted(weights_ref, part_ref[rows, :], rows)
        total = total + jnp.dot(turned_ref[:, rows], near, preferred_element_type=F32)
    sums_ref[...] = total
    gram_ref[:, :rank] = rough[:, :rank]
    gram_ref[:, rank:] = rest[:, :rank]


def middle_kernel(factors, oriented_ref, high_ref, gram_ref, sums_ref, send_ref, keep_high_ref, keep_low_ref):
    coeffs = own_coefficients(oriented_ref, 0, high_ref[...], factors)
    delta = jnp.dot(gram_ref[...], jnp.concatenate([coeffs] * 2, axis=0), preferred_element_type=F32)
    proj = sums_ref[...] + delta
    rank = high_ref.shape[0]
    send_ref[0] = proj[:rank]
    send_ref[1] = proj[rank : 2 * rank]
    keep_high_ref[...] = proj[2 * rank : 3 * rank]
    keep_low_ref[...] = proj[3 * rank :]


def second_part_kernel(
    factors, oriented_ref, high_ref, low_ref, high_other_ref, low_other_ref, bases_ref, part_ref, weights_ref, leaves_ref, out_ref, buf
):
    pieces = []
    order = []
    for slot, (own_ref, other_ref) in enumerate(((high_ref, high_other_ref), (low_ref, low_other_ref))):
        pieces += [own_coefficients(oriented_ref, slot, own_ref[...], factors)]
        pieces += [other_coefficients(oriented_ref, slot, other_ref[...], factors)]
        order += [own_level(slot), other_level(slot)]
    coeffs = jnp.concatenate(pieces, axis=0)
    for leaf in range(part_ref.shape[0] // LEAF):
        rows = slice(leaf * LEAF, (leaf + 1) * LEAF)
        basis = jnp.concatenate([bases_ref[level, rows, :] for level in order], axis=1)
        first = part_ref[rows, :] + jnp.dot(basis, coeffs, preferred_element_type=F32)
        buf[rows, :] = weighted(weights_ref, first, rows)
        out_ref[rows, :] = jnp.dot(leaves_ref[rows, :], buf[rows, :], preferred_element_type=F32)


def near_result_kernel(factors, oriented_ref, high_ref, low_ref, other_ref, bases_ref, part_ref, out_ref):
    pieces = [
        own_coefficients(oriented_ref, 0, high_ref[...], factors),
        own_coefficients(oriented_ref, 1, low_ref[...], factors),
        other_coefficients(oriented_ref, 1, other_ref[...], factors),
    ]
    order = [own_level(0), own_level(1), other_level(1)]
    basis = jnp.concatenate([bases_ref[level] for level in order], axis=1)
    coeffs = jnp.concatenate(pieces, axis=0)
    out_ref[...] = part_ref[...] + jnp.dot(basis, coeffs, preferred_element_type=F32)


def result_kernel(factors, oriented_ref, other_ref, bases_ref, part_ref, result_ref, buf, sems):
    coeffs = other_coefficients(oriented_ref, 0, other_ref[...], factors)
    copies = []
    for chunk in range(part_ref.shape[0] // CHUNK):
        rows = pl.ds(chunk * CHUNK, CHUNK)
        basis = bases_ref[other_level(0), rows, :]
        total = part_ref[rows, :] + jnp.dot(basis, coeffs, preferred_element_type=F32)
        buf[rows, :] = total.astype(BF16)
        copies.append(pltpu.make_async_copy(buf.at[rows, :], result_ref.at[rows, :], sems.at[chunk]))
        copies[-1].start()
    for copy in copies:
        copy.wait()


def on_device(signal, leaves, bases, couplings, weights):
    count = lax.axis_size(AXIS)
    bits = index_bits()
    rows_dev, width = signal.shape
    levels, _, rank = bases.shape
    odd = parity_of() == 1
    far1, far2, far3, far4 = (1 << (bits - level - 1) for level in range(levels))
    factors = [1.0 / math.sqrt(rows_dev * (count >> level + 1) * rank) for level in range(levels)]
    weight_rows = weights.reshape(rows_dev // SPAN, SPAN)
    mults = rows_dev * width * rank * 2
    chunks = rows_dev // CHUNK
    sums_shape = jax.ShapeDtypeStruct((rank, width), F32)
    pair_shape = jax.ShapeDtypeStruct((2, rank, width), F32)
    part_shape = jax.ShapeDtypeStruct((rows_dev, width), F32)
    gram_shape = jax.ShapeDtypeStruct((levels * rank, 2 * rank), F32)

    def swap(value, odd_mask, even_mask):
        pairs = [(source, source ^ (odd_mask if source % 2 else even_mask)) for source in range(count)]
        return lax.ppermute(value, AXIS, pairs)

    def beside(arrays, *riders):
        return lax.optimization_barrier((*arrays, *riders))

    def begin(got_high, got_low, high, low):
        high = high + got_high
        low = low + got_low
        for bit in range(1, bits - levels):
            high = high + swap(high, 1 << bit, 1 << bit)
            low = low + swap(low, 1 << bit, 1 << bit)
        return high, low

    def rounds(high, low, rider_one, rider_two, rider_three, passenger=None):
        near = swap(high, far1, far3)
        across = swap(high, far1 | far2, far4)
        near, across, *ridden = beside((near, across), *rider_one())
        high = jnp.where(odd, near + across, high + near)
        got = swap(high, far4, far2)
        low, passenger = beside((swap(low, far3, far4),), ridden.pop() if passenger is None else passenger)
        passenger = swap(passenger, 1, 1)
        got, *ridden = beside((got,), *rider_two(*ridden))
        high = jnp.where(odd, high + got, got)
        low = jnp.where(odd, low + swap(low, far4, far3), low)
        got = swap(high, far3, far4)
        got, *ridden = beside((got,), *rider_three(low, passenger, *ridden))
        return high + got, low, *ridden

    send_high, signal = call(
        first_kernel,
        [sums_shape, jax.ShapeDtypeStruct(signal.shape, BF16)],
        [pltpu.with_memory_space_constraint(array, pltpu.HBM) for array in (bases, signal)],
        mults,
        arrays_in=HBM,
        scratch=[pltpu.VMEM((rows_dev, rank), BF16), pltpu.SemaphoreType.DMA((2,))],
    )
    send_low, *kept = call(kept_kernel, [sums_shape] * 3, [bases, signal], 3 * mults)

    def first_riders():
        oriented, turned = call(
            prepare_kernel,
            [
                jax.ShapeDtypeStruct((levels, rank, rank), BF16),
                jax.ShapeDtypeStruct((levels * rank, rows_dev), BF16),
            ],
            [couplings, bases],
            mults,
        )
        keep, send = call(gram_kernel, [gram_shape] * 2, [bases, weight_rows, turned], 2 * levels * mults)
        return oriented, turned, keep, send

    def second_riders(oriented, turned, keep):
        (part,) = call(near_kernel, [part_shape], [leaves, signal], LEAF // rank * mults)
        return oriented, turned, keep, part

    def third_riders(low, got, oriented, turned, keep, part):
        sums, gram = call(
            functools.partial(low_kernel, factors),
            [
                jax.ShapeDtypeStruct((levels * rank, width), F32),
                jax.ShapeDtypeStruct((levels * rank, 2 * rank), BF16),
            ],
            [oriented, low, keep, got, part, weight_rows, turned],
            (1 + levels) * mults,
        )
        return oriented, part, sums, gram

    high, low, oriented, part, sums, gram = rounds(
        *begin(swap(send_high, 1, 1), swap(send_low, 1, 1), *kept), first_riders, second_riders, third_riders
    )
    high, low_other = beside((high, swap(low, 1, 1)))
    send, *kept = call(
        functools.partial(middle_kernel, factors),
        [pair_shape, sums_shape, sums_shape],
        [oriented, high, gram, sums],
        mults,
    )
    next_high, next_low, high, low = beside(begin(*swap(send, 1, 1), *kept), high, low)

    def second_part(_, high_other):
        return call(
            functools.partial(second_part_kernel, factors),
            [part_shape],
            [oriented, high, low, high_other, low_other, bases, part, weight_rows, leaves],
            (LEAF // rank + levels) * mults,
            scratch=[pltpu.VMEM((rows_dev, width), BF16)],
        )

    high, low, part = rounds(next_high, next_low, tuple, tuple, second_part, high)
    low_other, high_other = swap(low, 1, 1), swap(high, 1, 1)
    (part,) = call(
        functools.partial(near_result_kernel, factors),
        [part_shape],
        [oriented, high, low, low_other, bases, part],
        3 * mults,
    )
    (result,) = call(
        functools.partial(result_kernel, factors),
        [jax.ShapeDtypeStruct((rows_dev, width), BF16)],
        [oriented, high_other, bases, part],
        mults,
        outs_in=HBM,
        scratch=[pltpu.VMEM((rows_dev, width), BF16), pltpu.SemaphoreType.DMA((chunks,))],
    )
    return result


def solution(mesh):
    in_specs = (P("rows", None), P("rows", None), P(None, "rows", None), P(), P("rows"))
    out_specs = P("rows", None)
    return jax.shard_map(
        on_device, mesh=mesh, in_specs=in_specs, out_specs=out_specs, check_vma=False
    )
```
